512 devices in a mesh: bank: 256 (over x, y, z), det: 2 (over core).
Axes of the slice: x: 4, y: 4, z: 16, core: 2. Of those that a mesh axis runs over, the one named last changes fastest.
Arguments:
- strain: float32 [2, 2, 65536], P('det', None, 'bank'), may hold values from -6 to 6
- asd_inv: float32 [2, 65536], P('det', 'bank'), may hold values from 0.5 to 2
- indices: int32 [4096], P('bank'), may hold values from 0 to 16383
- counts: int32 [256], P('bank'), may hold values from 1 to 16, as said below
- sky_delay: int32 [16], replicated, may hold values from -21 to 21, as said below
- gain_near: float32 [16], replicated, may hold values from 0.2 to 1
- gain_far: float32 [16], replicated, may hold values from -1 to 1
Outputs:
- coherent: float32 [4096, 16, 4096], P('bank', None, 'det')
The draws below stay inside these ranges and needn't reach their ends.
Inputs may be any that keep to these rules, and one draw needn't show every extreme that they name: `counts`: filled slots of each bank index; some bank index fills all 16. `sky_delay`: both extreme delays occur.
All inputs are finite; a program needn't handle non-finite values.
Results may differ from the reference program's by a relative error of at most 0.01.
Values may be sent and summed in bfloat16 or wider, within the bound.
No kernel may reach another device: no remote copies, remote signals or barrier semaphores. Data moves between devices by JAX's collectives and lax.ppermute only.
A program may use at most 64 MiB of HBM per device.

```python
import math
import jax
import jax.numpy as jnp
from jax import lax

DFT_ROWS = 512
DFT_COLS = 256
SAMPLES = 131072
BINS = 65536
LOW_BIN = 1920
WIN_BLOCKS = 8
WINDOW = 4096
TPL_DEV = 16
TEMPLATES = 4096
SKY = 16
MAX_DELAY = 21
BANK_TABLE = 16384
N_BANK = 256
N_DET = 2


def draw_counts(key, part):
    key = jax.random.fold_in(key, 11)
    first_key, second_key = jax.random.split(key)
    random_draw = jax.random.randint(first_key, (N_BANK,), 0, TPL_DEV)
    skewed = 1 + random_draw * random_draw // TPL_DEV
    full_slot = jax.random.randint(second_key, (), 0, N_BANK)
    return jnp.where(jnp.arange(N_BANK) == full_slot, TPL_DEV, skewed).astype(jnp.int32)


def draw_sky_delay(key, part):
    key = jax.random.fold_in(key, 23)
    first_key, second_key, third_key = jax.random.split(key, 3)
    lags = jax.random.randint(first_key, (SKY,), -MAX_DELAY, MAX_DELAY + 1)
    low_place = jax.random.randint(second_key, (), 0, SKY)
    high_place = (low_place + 1 + jax.random.randint(third_key, (), 0, SKY - 1)) % SKY
    positions = jnp.arange(SKY)
    lags = jnp.where(positions == low_place, -MAX_DELAY, lags)
    lags = jnp.where(positions == high_place, MAX_DELAY, lags)
    return lags.astype(jnp.int32)


def set_ends(values, rng, smallest, high):
    dims = values.shape
    spot = [jax.random.randint(jax.random.fold_in(rng, axis), (), 0, dims[axis]) for axis in range(len(dims))]
    values = values.at[tuple(spot)].set(smallest)
    longest = dims.index(max(dims))
    spot[longest] = (spot[longest] + 1) % dims[longest]
    return values.at[tuple(spot)].set(high)


def levels(rng, shape, pieces, low, high):
    factor_of, own = 1.0, jax.random.fold_in(rng, 6)
    for position, blocks in pieces:
        draws = jnp.exp(jax.random.uniform(jax.random.fold_in(own, position), (blocks,), jnp.float32, low / len(pieces), high / len(pieces)))
        factor_of = factor_of * jnp.repeat(draws, shape[position] // blocks).reshape([-1 if axis == position else 1 for axis in range(len(shape))])
    return factor_of


def bell_draw(rng, shape, spread, most, cuts=(), kind=jnp.bfloat16):
    drawn = jax.random.normal(rng, shape, jnp.float32) * spread
    if len(cuts) > 0:
        drawn = levels(rng, shape, cuts, -0.22, 0.18) * drawn
    return jnp.clip(drawn, min=-most, max=most).astype(kind)


def setup_inputs(seed: int = 0) -> dict:
    key_list = jax.random.split(jax.random.key(seed), 8)
    return {
        "strain": bell_draw(key_list[0], (N_DET, 2, BINS), 1.0, 6.0, ((0, 2), (2, 256)), jnp.float32),
        "asd_inv": jnp.clip(jnp.exp(math.log(2.0) - 1.3862944 * jax.random.uniform(key_list[1], (N_DET, BINS), jnp.float32) ** levels(key_list[1], (N_DET, BINS), ((0, 2), (1, 256)), -0.2, 0.2)), 0.5, 2.0),
        "indices": set_ends(jax.random.randint(key_list[2], (TEMPLATES,), 0, BANK_TABLE), jax.random.fold_in(key_list[2], 1), 0, BANK_TABLE - 1).astype(jnp.int32),
        "counts": draw_counts(jax.random.fold_in(key_list[7], 71), 0),
        "sky_delay": draw_sky_delay(jax.random.fold_in(key_list[7], 71), 0),
        "gain_near": jnp.clip(jax.random.uniform(key_list[5], (SKY,), jnp.float32, 0.2, 1.0), 0.2, 1.0),
        "gain_far": jnp.clip(jax.random.uniform(key_list[6], (SKY,), jnp.float32, -1.0, 1.0), -1.0, 1.0),
    }


MSUN_SEC = 4.925491e-06
SAMPLE_RATE = 2048.0

def template_terms(table_index):
    total_mass = 6.0 * jnp.power(1.03, (table_index % 64).astype(jnp.float32))
    sym_ratio = 0.16 + 0.09 * (table_index // 64 % 64).astype(jnp.float32) / 63.0
    spin_value = -0.6 + 0.4 * (table_index // 4096).astype(jnp.float32)
    seconds = total_mass * MSUN_SEC
    return (seconds, sym_ratio, spin_value * (113.0 - 76.0 * sym_ratio) / 12.0)

def amplitude(seconds, frequency):
    clipped = jnp.maximum(frequency, 1.0)
    cutoff = 1.0 / (6.0 ** 1.5 * math.pi * seconds)
    scaled = clipped / cutoff
    return clipped ** (-7.0 / 6.0) * jnp.exp(-(scaled * scaled) * (scaled * scaled))

def phase(seconds, sym_ratio, orbit_term, frequency):
    clipped = jnp.maximum(frequency, 1.0)
    velocity = (math.pi * seconds * clipped) ** (1.0 / 3.0)
    square = velocity * velocity
    leading = 3.0 / (128.0 * sym_ratio * square * square * velocity)
    series_terms = 1.0 + (3715.0 / 756.0 + 55.0 * sym_ratio / 9.0) * square + (4.0 * orbit_term - 16.0 * math.pi) * square * velocity
    return leading * series_terms - math.pi / 4.0

def transform_tables():
    rows_t = jnp.arange(DFT_ROWS)[:, None]
    cols_k = jnp.arange(DFT_ROWS // 2)[None, :]
    angle_one = 2.0 * math.pi / DFT_ROWS * (rows_t * cols_k % DFT_ROWS).astype(jnp.float32)
    cosine_one = jnp.cos(angle_one).astype(jnp.bfloat16)
    sine_one = jnp.sin(angle_one).astype(jnp.bfloat16)
    first_table = jnp.concatenate([jnp.concatenate([cosine_one, -sine_one], 1), jnp.concatenate([sine_one, cosine_one], 1)], 0)
    twist_bins = jnp.arange(DFT_COLS)[None, :]
    angle_two = 2.0 * math.pi / SAMPLES * (rows_t * twist_bins % SAMPLES).astype(jnp.float32)
    twist_cos = jnp.cos(angle_two)
    twist_sin = jnp.sin(angle_two)
    inner_k = jnp.arange(DFT_COLS)[:, None]
    column_t = DFT_COLS // 2 - WIN_BLOCKS // 2 - 1 + jnp.arange(WIN_BLOCKS + 2)[None, :]
    angle_three = 2.0 * math.pi / DFT_COLS * (inner_k * column_t % DFT_COLS).astype(jnp.float32)
    cosine_three = jnp.cos(angle_three).astype(jnp.bfloat16)
    sine_three = jnp.sin(angle_three).astype(jnp.bfloat16)
    last_table = jnp.concatenate([jnp.concatenate([cosine_three, sine_three], 1), jnp.concatenate([-sine_three, cosine_three], 1)], 0)
    return (first_table, twist_cos, twist_sin, last_table)

def filter_template(over_white, envelope, phase_angle, tables):
    first_table, twist_cos, twist_sin, last_table = tables
    cosine = envelope * jnp.cos(phase_angle)
    sine = envelope * jnp.sin(phase_angle)
    real_part = over_white[0] * cosine - over_white[1] * sine
    imag_part = over_white[0] * sine + over_white[1] * cosine
    stacked = jnp.concatenate([real_part.reshape(DFT_ROWS // 2, DFT_COLS), imag_part.reshape(DFT_ROWS // 2, DFT_COLS)], 0).astype(jnp.bfloat16)
    middle = jnp.dot(first_table, stacked, preferred_element_type=jnp.float32)
    upper = middle[:DFT_ROWS]
    lower = middle[DFT_ROWS:]
    twisted = jnp.concatenate([upper * twist_cos - lower * twist_sin, upper * twist_sin + lower * twist_cos], 1).astype(jnp.bfloat16)
    result = jnp.dot(twisted, last_table, preferred_element_type=jnp.float32)
    width = WIN_BLOCKS + 2
    return jnp.stack([result[:, :width].T.reshape(-1), result[:, width:].T.reshape(-1)])

def coherent_stat(first_win, second_win, offset, length, delays, gain_near, gain_far):
    near_part = first_win[..., offset:offset + length].astype(jnp.float32)

    def per_sky(lag_samples, weight_near, weight_far):
        far_part = lax.dynamic_slice_in_dim(second_win, offset + lag_samples, length, second_win.ndim - 1).astype(jnp.float32)
        real_part = weight_near * near_part[..., 0, :] + weight_far * far_part[..., 0, :]
        imag_part = weight_near * near_part[..., 1, :] + weight_far * far_part[..., 1, :]
        return (real_part * real_part + imag_part * imag_part) / (weight_near * weight_near + weight_far * weight_far)
    return jax.vmap(per_sky, in_axes=(0, 0, 0), out_axes=-2)(delays, gain_near, gain_far)

def reference(strain, asd_inv, indices, counts, sky_delay, gain_near, gain_far):
    weight_sq = asd_inv * asd_inv
    over_white = strain * weight_sq[:, None, :]
    bin_ids = jnp.arange(BINS)
    frequency = bin_ids.astype(jnp.float32) * (SAMPLE_RATE / SAMPLES)
    tables = transform_tables()

    def filter_slot(slot_id):
        table_index = indices[slot_id]
        active = slot_id % TPL_DEV < counts[slot_id // TPL_DEV]

        def compute(unused):
            seconds, sym_ratio, orbit_term = template_terms(table_index)
            envelope = jnp.where(bin_ids >= LOW_BIN, amplitude(seconds, frequency), 0.0)
            phase_angle = phase(seconds, sym_ratio, orbit_term, frequency)
            per_det = []
            for det_index in range(2):
                norm_sq = jnp.sum(envelope * envelope * weight_sq[det_index])
                filtered = filter_template(over_white[det_index], envelope, phase_angle, tables)
                per_det.append((filtered / jnp.sqrt(norm_sq)).astype(jnp.bfloat16))
            return coherent_stat(per_det[0], per_det[1], DFT_ROWS, WINDOW, sky_delay, gain_near, gain_far)

        def empty_slot(unused):
            return jnp.zeros((SKY, WINDOW), jnp.float32)
        return lax.cond(active, compute, empty_slot, 0)
    return lax.map(filter_slot, jnp.arange(TEMPLATES))
```

```python
import math

import jax
import jax.numpy as jnp
import numpy as np
from jax import lax
from jax.experimental import pallas as pl
from jax.experimental.pallas import tpu as pltpu
from jax.sharding import PartitionSpec as P

DFT_ROWS = 512
DFT_COLS = 256
SAMPLES = 131072
LOW_BIN = 1920
WIN_BLOCKS = 8
WINDOW = 4096
HALF = WINDOW // 2
TPL_DEV = 16
SKY = 16
MASSES = 64
N_Z = 16
N_XY = 16
COLS = WIN_BLOCKS + 2
SPAN = HALF + 256
PAYLOAD = 640
STRIP = 32
TIME_BLOCK = 512

MSUN_SEC = 4.925491e-06
SAMPLE_RATE = 2048.0

Z_ORDER = [8, 10, 12, 14, 0, 2, 4, 6, 9, 11, 13, 15, 1, 3, 5, 7]
XY_ORDER = [(k + 5) % N_XY for k in range(N_XY)]


def group_lists():
    z_groups = [[q * N_Z + z for z in Z_ORDER] for q in range(N_XY)]
    xy_groups = [[q * N_Z + z for q in XY_ORDER] for z in range(N_Z)]
    return z_groups, xy_groups


def constant_tables():
    rows = np.array([[q * N_Z + z for z in Z_ORDER] for q in XY_ORDER])
    even, odd = rows[:, :8].reshape(-1), rows[:, 8:].reshape(-1)
    k1 = np.concatenate([even, odd])
    k2 = np.arange(DFT_COLS)
    bins = 256 * k1[None, :] + k2[:, None]
    freq = np.maximum(bins * (SAMPLE_RATE / SAMPLES), 1.0)
    powers = np.stack(
        [
            freq ** (-5.0 / 3.0),
            freq**-1.0,
            freq ** (-2.0 / 3.0),
            np.where(bins >= LOW_BIN, freq ** (-7.0 / 6.0), 0.0),
            freq**4,
        ]
    ).astype(np.float32)

    t1 = np.arange(256)

    def first(rows_k):
        angle = 2.0 * np.pi / 512 * (rows_k[:, None] * t1[None, :] % 512)
        c, s = np.cos(angle), np.sin(angle)
        return np.concatenate([np.concatenate([c, s], 1), np.concatenate([-s, c], 1)], 0)

    first_tables = np.stack([first(even), first(odd)])
    t_all = np.arange(512)
    angle = 2.0 * np.pi / SAMPLES * (k2[:, None] * t_all[None, :] % SAMPLES)
    twist = np.stack([np.cos(angle), np.sin(angle)]).astype(np.float32)
    t2 = DFT_COLS // 2 - WIN_BLOCKS // 2 - 1 + np.arange(COLS)
    angle = 2.0 * np.pi / DFT_COLS * (t2[:, None] * k2[None, :] % DFT_COLS)
    c, s = np.cos(angle), np.sin(angle)
    last = np.zeros((32, 512))
    last[:COLS] = np.concatenate([c, -s], 1)
    last[COLS : 2 * COLS] = np.concatenate([s, c], 1)

    seconds = 6.0 * 1.03 ** np.arange(MASSES) * MSUN_SEC
    ratio = 0.16 + 0.09 * np.arange(64) / 63.0
    x = np.pi * seconds
    turn = 1.0 / (2.0 * np.pi)
    scalars = np.stack(
        [
            turn * x ** (-5.0 / 3.0),
            turn * x**-1.0,
            turn * x ** (-2.0 / 3.0),
            -((6.0**1.5 * x) ** 4) / math.log(2.0),
            3.0 / (128.0 * ratio),
            3715.0 / 756.0 + 55.0 * ratio / 9.0,
            (113.0 - 76.0 * ratio) / 12.0,
            np.zeros(64),
        ]
    ).astype(np.float32)
    return (
        powers,
        first_tables.astype(jnp.bfloat16),
        twist,
        last.astype(jnp.bfloat16),
        scalars,
    )


def even_fit(function, terms):
    nodes = 0.5 * np.cos(np.pi * (np.arange(400) + 0.5) / 400)
    design = (nodes[:, None] ** 2) ** np.arange(terms)[None, :]
    fitted = np.linalg.lstsq(design, function(nodes), rcond=None)[0]
    return [float(np.float32(v)) for v in fitted]


ROOT2 = math.sqrt(2.0)
SIN_FIT = even_fit(lambda r: ROOT2 * np.pi * np.sinc(r), 5)
COS_FIT = even_fit(lambda r: ROOT2 * np.cos(np.pi * r), 5)
ROUND_SHIFT = 12582912.0


def horner(coefs, square):
    total = coefs[-1] * square + coefs[-2]
    for c in coefs[-3::-1]:
        total = total * square + c
    return total


def prepare_kernel(bank_ref, strain_ref, asd_ref, out_ref):
    weight = asd_ref[...] * asd_ref[...]
    over = strain_ref[...] * weight
    bin_id = bank_ref[0] * 256 + lax.broadcasted_iota(jnp.int32, (1, 256), 1)
    clipped = jnp.maximum(bin_id.astype(jnp.float32) * (SAMPLE_RATE / SAMPLES), 1.0)
    square = clipped * clipped
    weighted = jnp.where(
        bin_id >= LOW_BIN, jnp.exp((-7.0 / 3.0) * jnp.log(clipped)), 0.0
    ) * weight
    mass_id = lax.broadcasted_iota(jnp.int32, (MASSES, 1), 0).astype(jnp.float32)
    start = math.log(2.0) + 4.0 * math.log(6.0**1.5 * math.pi * 6.0 * MSUN_SEC)
    steep = jnp.exp(4.0 * math.log(1.03) * mass_id + start)
    terms = jnp.exp(-steep * (square * square)) * weighted
    column = jnp.sum(terms, axis=1, keepdims=True)
    row_id = lax.broadcasted_iota(jnp.int32, (MASSES, MASSES), 0)
    col_id = lax.broadcasted_iota(jnp.int32, (MASSES, MASSES), 1)
    norms = jnp.sum(jnp.where(row_id == col_id, column, 0.0), axis=0, keepdims=True)
    coarse = norms.astype(jnp.bfloat16).astype(jnp.float32)
    row = jnp.concatenate(
        [over[0:1].astype(jnp.bfloat16).astype(jnp.float32), over[1:2].astype(jnp.bfloat16).astype(jnp.float32), coarse, norms - coarse], axis=1
    )
    out_ref[...] = jnp.broadcast_to(row[:, None, :], (N_Z, 1, PAYLOAD))


def filter_kernel(
    indices_ref,
    counts_ref,
    half_ref,
    scalars_ref,
    gathered_ref,
    powers_ref,
    first_ref,
    twist_ref,
    last_ref,
    own_ref,
    send_ref,
    spectrum,
    products,
    middle,
    twisted,
    series,
):
    count = counts_ref[0]
    for part in range(2):
        block = gathered_ref[:, :, 256 * part : 256 * part + 256].astype(jnp.float32)
        for parity in range(2):
            rows = block[:, 8 * parity : 8 * parity + 8].reshape(128, 256)
            spectrum[part, :, 128 * parity : 128 * parity + 128] = rows.T
    sums = jnp.sum(gathered_ref[:, :, 512:640].astype(jnp.float32).reshape(256, 128), axis=0, keepdims=True)
    norm_row = sums[:, :MASSES] + sums[:, MASSES:]
    lane_id = lax.broadcasted_iota(jnp.int32, (1, MASSES), 1)
    series[...] = jnp.zeros_like(series)

    @pl.loop(0, count)
    def _(slot):
        entry = indices_ref[slot]
        mass, eta = entry % 64, entry // 64 % 64
        spin = -0.6 + 0.4 * (entry // 4096).astype(jnp.float32)
        lead = scalars_ref[4, eta]
        c53 = lead * scalars_ref[0, mass]
        c1 = lead * scalars_ref[5, eta] * scalars_ref[1, mass]
        c23 = lead * (4.0 * spin * scalars_ref[6, eta] - 16.0 * math.pi) * scalars_ref[2, mass]
        steep = scalars_ref[3, mass]
        norm = jnp.sum(jnp.where(lane_id == mass, norm_row, 0.0), axis=1, keepdims=True)
        scale = lax.rsqrt(norm)

        @pl.loop(0, DFT_COLS // STRIP)
        def _(strip):
            here = pl.ds(pl.multiple_of(strip * STRIP, STRIP), STRIP)
            turns = (
                c53 * powers_ref[0, here, :]
                + c1 * powers_ref[1, here, :]
                + (c23 * powers_ref[2, here, :] - 0.125)
            )
            rest = turns - ((turns + ROUND_SHIFT) - ROUND_SHIFT)
            square = rest * rest
            half_sin = horner(SIN_FIT, square) * rest
            half_cos = horner(COS_FIT, square)
            envelope = powers_ref[3, here, :] * jnp.exp2(steep * powers_ref[4, here, :])
            sine = envelope * (half_sin * half_cos)
            cosine = envelope * (1.0 - half_sin * half_sin)
            re, im = spectrum[0, here, :], spectrum[1, here, :]
            real_part = (re * cosine - im * sine).astype(jnp.bfloat16)
            imag_part = (re * sine + im * cosine).astype(jnp.bfloat16)
            for parity in range(2):
                lanes = slice(128 * parity, 128 * parity + 128)
                products[parity, here, 0:128] = real_part[:, lanes]
                products[parity, here, 128:256] = imag_part[:, lanes]

        for parity in range(2):
            middle[parity] = jnp.dot(
                products[parity], first_ref[parity], preferred_element_type=jnp.float32
            )

        @pl.loop(0, DFT_COLS // STRIP)
        def _(strip):
            base = pl.multiple_of(strip * STRIP, STRIP)
            here, below = pl.ds(base, STRIP), pl.ds(base + DFT_COLS, STRIP)
            for side in range(2):
                lanes = slice(256 * side, 256 * side + 256)
                if side == 0:
                    upper = middle[0, here, 0:256] + middle[1, here, 0:256]
                    lower = middle[0, here, 256:512] + middle[1, here, 256:512]
                else:
                    upper = middle[0, here, 0:256] - middle[1, here, 0:256]
                    lower = middle[0, here, 256:512] - middle[1, here, 256:512]
                c, s = twist_ref[0, here, lanes], twist_ref[1, here, lanes]
                twisted[here, lanes] = (upper * c - lower * s).astype(jnp.bfloat16)
                twisted[below, lanes] = (upper * s + lower * c).astype(jnp.bfloat16)

        result = jnp.dot(last_ref[...], twisted[...], preferred_element_type=jnp.float32)
        scaled = result[: 2 * COLS] * scale
        for i in range(4):
            series[i, pl.ds(slot, 2 * COLS, stride=TPL_DEV), :] = scaled[:, 128 * i : 128 * i + 128]

    def write(out_ref, half):
        for part in range(2):
            start = (part * COLS + 4 * half) * TPL_DEV

            def rows(column):
                return pl.ds(pl.multiple_of(start + column * TPL_DEV, TPL_DEV), TPL_DEV)

            for i in range(SPAN // 128):
                column, tile = divmod(i + 3, 4)
                out_ref[part, :, 128 * i : 128 * i + 128] = series[tile, rows(column), :].astype(
                    jnp.bfloat16
                )

    write(own_ref, half_ref[0])
    write(send_ref, 1 - half_ref[0])


def coherent_kernel(half_ref, delay_ref, near_gain_ref, far_gain_ref, own_ref, got_ref, out_ref, near, far, tiles):
    block = pl.program_id(0)

    def unpack(near_ref, far_ref):
        for part in range(2):
            near[part] = near_ref[part, :, 128 : 128 + HALF].astype(jnp.float32)
            far[part] = far_ref[part].astype(jnp.float32)[:, 64 : 64 + HALF + 128]

    @pl.when((block == 0) & (half_ref[0] == 0))
    def _():
        unpack(own_ref, got_ref)

    @pl.when((block == 0) & (half_ref[0] == 1))
    def _():
        unpack(got_ref, own_ref)

    lane_id = lax.broadcasted_iota(jnp.int32, (TPL_DEV, 128), 1)
    first_lane = pl.multiple_of(block * TIME_BLOCK, 128)

    @pl.loop(0, SKY)
    def _(sky):
        shift = delay_ref[sky] + 64
        gain_near = near_gain_ref[sky]
        gain_far = far_gain_ref[sky]
        power = jnp.full((1, 128), gain_near * gain_near + gain_far * gain_far, jnp.float32)
        inverse = 1.0 / power
        keep = lane_id < 128 - shift
        total = [None] * (TIME_BLOCK // 128)
        for part in range(2):
            rolled = [
                pltpu.roll(far[part, :, pl.ds(first_lane + 128 * i, 128)], 128 - shift, axis=1)
                for i in range(TIME_BLOCK // 128 + 1)
            ]
            for i in range(TIME_BLOCK // 128):
                shifted = jnp.where(keep, rolled[i], rolled[i + 1])
                mixed = (
                    gain_near * near[part, :, pl.ds(first_lane + 128 * i, 128)] + gain_far * shifted
                )
                squared = mixed * mixed
                total[i] = squared if part == 0 else total[i] + squared
        for i in range(TIME_BLOCK // 128):
            tiles[i, pl.ds(sky, TPL_DEV, stride=SKY), :] = total[i] * inverse

    for i in range(TIME_BLOCK // 128):
        out_ref[:, 128 * i : 128 * i + 128] = tiles[i]


VMEM = pl.BlockSpec(memory_space=pltpu.VMEM)
SMEM = pl.BlockSpec(memory_space=pltpu.SMEM)


def on_device(strain, asd_inv, indices, counts, sky_delay, gain_near, gain_far):
    powers, first_tables, twist, last, scalars = constant_tables()
    z_groups, xy_groups = group_lists()
    bank = lax.axis_index("bank").astype(jnp.int32)[None]
    half = lax.axis_index("det").astype(jnp.int32)[None]
    payload = pl.pallas_call(
        prepare_kernel,
        out_shape=jax.ShapeDtypeStruct((N_Z, 1, PAYLOAD), jnp.float32),
        in_specs=[SMEM, VMEM, VMEM],
        out_specs=VMEM,
    )(bank, strain[0], asd_inv)
    line = lax.all_to_all(payload, "bank", 0, 0, axis_index_groups=z_groups)
    line = line.reshape(N_Z, PAYLOAD).astype(jnp.bfloat16)
    plane = lax.all_to_all(
        jnp.broadcast_to(line[None], (N_XY, N_Z, PAYLOAD)), "bank", 0, 0, axis_index_groups=xy_groups
    )
    window = jax.ShapeDtypeStruct((2, TPL_DEV, SPAN), jnp.bfloat16)
    own, send = pl.pallas_call(
        filter_kernel,
        out_shape=(window, window),
        in_specs=[SMEM] * 4 + [VMEM] * 5,
        out_specs=(VMEM, VMEM),
        scratch_shapes=[
            pltpu.VMEM((2, DFT_COLS, 256), jnp.float32),
            pltpu.VMEM((2, DFT_COLS, 256), jnp.bfloat16),
            pltpu.VMEM((2, DFT_COLS, 512), jnp.float32),
            pltpu.VMEM((512, 512), jnp.bfloat16),
            pltpu.VMEM((4, 2 * COLS * TPL_DEV, 128), jnp.float32),
        ],
        compiler_params=pltpu.CompilerParams(vmem_limit_bytes=40 * 1024 * 1024),
    )(indices, counts, half, scalars, plane, powers, first_tables, twist, last)
    got = lax.ppermute(send, "det", [(0, 1), (1, 0)])
    out = pl.pallas_call(
        coherent_kernel,
        grid=(HALF // TIME_BLOCK,),
        out_shape=jax.ShapeDtypeStruct((TPL_DEV * SKY, HALF), jnp.float32),
        in_specs=[SMEM] * 4 + [VMEM] * 2,
        out_specs=pl.BlockSpec((TPL_DEV * SKY, TIME_BLOCK), lambda t: (0, t)),
        scratch_shapes=[
            pltpu.VMEM((2, TPL_DEV, HALF), jnp.float32),
            pltpu.VMEM((2, TPL_DEV, HALF + 128), jnp.float32),
            pltpu.VMEM((TIME_BLOCK // 128, TPL_DEV * SKY, 128), jnp.float32),
        ],
        compiler_params=pltpu.CompilerParams(vmem_limit_bytes=40 * 1024 * 1024),
    )(half, sky_delay, gain_near, gain_far, own, got)
    return out.reshape(TPL_DEV, SKY, HALF)


def solution(mesh):
    return jax.shard_map(
        on_device,
        mesh=mesh,
        in_specs=(P("det", None, "bank"), P("det", "bank"), P("bank"), P("bank"), P(), P(), P()),
        out_specs=P("bank", None, "det"),
        check_vma=False,
    )
```

```python
import math

import jax
import jax.numpy as jnp
import numpy as np
from jax import lax
from jax.experimental import pallas as pl
from jax.experimental.pallas import tpu as pltpu
from jax.sharding import PartitionSpec as P

DFT_ROWS = 512
DFT_COLS = 256
SAMPLES = 131072
LOW_BIN = 1920
WIN_BLOCKS = 8
WINDOW = 4096
HALF = WINDOW // 2
TPL_DEV = 16
SKY = 16
MASSES = 64
N_Z = 16
N_XY = 16
COLS = WIN_BLOCKS + 2
SPAN = HALF + 256
PAYLOAD = 640
STRIP = 16
BATCH = 4
TILES = HALF // 128
GROUP = 4

MSUN_SEC = 4.925491e-06
SAMPLE_RATE = 2048.0

Z_ORDER = [8, 10, 12, 14, 0, 2, 4, 6, 9, 11, 13, 15, 1, 3, 5, 7]
XY_ORDER = [(k + 5) % N_XY for k in range(N_XY)]


def group_lists():
    z_groups = [[q * N_Z + z for z in Z_ORDER] for q in range(N_XY)]
    xy_groups = [[q * N_Z + z for q in XY_ORDER] for z in range(N_Z)]
    return z_groups, xy_groups


def constant_tables():
    rows = np.array([[q * N_Z + z for z in Z_ORDER] for q in XY_ORDER])
    even, odd = rows[:, :8].reshape(-1), rows[:, 8:].reshape(-1)
    k1 = np.concatenate([even, odd])
    k2 = np.arange(DFT_COLS)
    bins = 256 * k1[None, :] + k2[:, None]
    freq = np.maximum(bins * (SAMPLE_RATE / SAMPLES), 1.0)
    powers = np.stack(
        [
            freq ** (-5.0 / 3.0),
            freq**-1.0,
            freq ** (-2.0 / 3.0),
            np.where(bins >= LOW_BIN, freq ** (-7.0 / 6.0), 0.0),
            freq**4,
        ]
    ).astype(np.float32)

    t1 = np.arange(256)

    def first(rows_k):
        angle = 2.0 * np.pi / 512 * (rows_k[:, None] * t1[None, :] % 512)
        c, s = np.cos(angle), np.sin(angle)
        return np.concatenate([np.concatenate([c, s], 1), np.concatenate([-s, c], 1)], 0)

    first_tables = np.stack([first(even), first(odd)])
    angle = 2.0 * np.pi / SAMPLES * (k2[:, None] * t1[None, :] % SAMPLES)
    twist = np.stack([np.cos(angle), np.sin(angle)]).astype(np.float32)
    t2 = DFT_COLS // 2 - WIN_BLOCKS // 2 - 1 + np.arange(COLS)
    last = np.zeros((2, 32, 512))
    for side in range(2):
        steps = k2[None, :] * (t2[:, None] * DFT_ROWS + 256 * side)
        angle = 2.0 * np.pi / SAMPLES * (steps % SAMPLES)
        c, s = np.cos(angle), np.sin(angle)
        last[side, :COLS] = np.concatenate([c, -s], 1)
        last[side, COLS : 2 * COLS] = np.concatenate([s, c], 1)

    seconds = 6.0 * 1.03 ** np.arange(MASSES) * MSUN_SEC
    ratio = 0.16 + 0.09 * np.arange(64) / 63.0
    x = np.pi * seconds
    turn = 1.0 / (2.0 * np.pi)
    scalars = np.stack(
        [
            turn * x ** (-5.0 / 3.0),
            turn * x**-1.0,
            turn * x ** (-2.0 / 3.0),
            -((6.0**1.5 * x) ** 4) / math.log(2.0),
            3.0 / (128.0 * ratio),
            3715.0 / 756.0 + 55.0 * ratio / 9.0,
            (113.0 - 76.0 * ratio) / 12.0,
            np.zeros(64),
        ]
    ).astype(np.float32)
    return (
        powers,
        first_tables.astype(jnp.bfloat16),
        twist,
        last.astype(jnp.bfloat16),
        scalars,
    )


def even_fit(function, terms):
    nodes = 0.5 * np.cos(np.pi * (np.arange(400) + 0.5) / 400)
    design = (nodes[:, None] ** 2) ** np.arange(terms)[None, :]
    fitted = np.linalg.lstsq(design, function(nodes), rcond=None)[0]
    return [float(np.float32(v)) for v in fitted]


ROOT2 = math.sqrt(2.0)
SIN_FIT = even_fit(lambda r: ROOT2 * np.pi * np.sinc(r), 5)
COS_FIT = even_fit(lambda r: ROOT2 * np.cos(np.pi * r), 5)
ROUND_SHIFT = 12582912.0


def horner(coefs, square):
    total = coefs[-1] * square + coefs[-2]
    for c in coefs[-3::-1]:
        total = total * square + c
    return total


def prepare_kernel(bank_ref, strain_ref, asd_ref, out_ref):
    weight = asd_ref[...] * asd_ref[...]
    over = strain_ref[...] * weight
    bin_id = bank_ref[0] * 256 + lax.broadcasted_iota(jnp.int32, (1, 256), 1)
    clipped = jnp.maximum(bin_id.astype(jnp.float32) * (SAMPLE_RATE / SAMPLES), 1.0)
    square = clipped * clipped
    weighted = jnp.where(
        bin_id >= LOW_BIN, jnp.exp((-7.0 / 3.0) * jnp.log(clipped)), 0.0
    ) * weight
    mass_id = lax.broadcasted_iota(jnp.int32, (MASSES, 1), 0).astype(jnp.float32)
    start = math.log(2.0) + 4.0 * math.log(6.0**1.5 * math.pi * 6.0 * MSUN_SEC)
    steep = jnp.exp(4.0 * math.log(1.03) * mass_id + start)
    terms = jnp.exp(-steep * (square * square)) * weighted
    column = jnp.sum(terms, axis=1, keepdims=True)
    row_id = lax.broadcasted_iota(jnp.int32, (MASSES, MASSES), 0)
    col_id = lax.broadcasted_iota(jnp.int32, (MASSES, MASSES), 1)
    norms = jnp.sum(jnp.where(row_id == col_id, column, 0.0), axis=0, keepdims=True)
    coarse = norms.astype(jnp.bfloat16).astype(jnp.float32)
    row = jnp.concatenate(
        [over[0:1].astype(jnp.bfloat16).astype(jnp.float32), over[1:2].astype(jnp.bfloat16).astype(jnp.float32), coarse, norms - coarse], axis=1
    )
    out_ref[...] = jnp.broadcast_to(row[:, None, :], (N_Z, 1, PAYLOAD))


def spread_kernel(line_ref, out_ref):
    line = line_ref[...].reshape(N_Z, PAYLOAD).astype(jnp.bfloat16)
    for i in range(N_XY):
        out_ref[i] = line


def wave_kernel(indices_ref, counts_ref, scalars_ref, powers_ref, waves_ref):
    @pl.loop(0, (counts_ref[0] + BATCH - 1) // BATCH * BATCH)
    def _(slot):
        entry = indices_ref[slot]
        mass, eta = entry % 64, entry // 64 % 64
        spin = -0.6 + 0.4 * (entry // 4096).astype(jnp.float32)
        lead = scalars_ref[4, eta]
        c53 = lead * scalars_ref[0, mass]
        c1 = lead * scalars_ref[5, eta] * scalars_ref[1, mass]
        c23 = lead * (4.0 * spin * scalars_ref[6, eta] - 16.0 * math.pi) * scalars_ref[2, mass]
        steep = scalars_ref[3, mass]

        @pl.loop(0, DFT_COLS // 64)
        def _(strip):
            for step in range(8):
                here = pl.ds(pl.multiple_of(strip * 64 + step * 8, 8), 8)
                turns = (
                    c53 * powers_ref[0, here, :]
                    + c1 * powers_ref[1, here, :]
                    + (c23 * powers_ref[2, here, :] - 0.125)
                )
                rest = turns - ((turns + ROUND_SHIFT) - ROUND_SHIFT)
                square = rest * rest
                half_sin = horner(SIN_FIT, square) * rest
                half_cos = horner(COS_FIT, square)
                envelope = powers_ref[3, here, :] * jnp.exp2(steep * powers_ref[4, here, :])
                waves_ref[slot, 0, here, :] = envelope * (1.0 - half_sin * half_sin)
                waves_ref[slot, 1, here, :] = envelope * (half_sin * half_cos)


def filter_kernel(
    indices_ref,
    counts_ref,
    half_ref,
    waves_ref,
    gathered_ref,
    first_ref,
    twist_ref,
    last_ref,
    own_ref,
    send_ref,
    spectrum,
    products,
    middle,
    twisted,
    series,
):
    count = counts_ref[0]
    for part in range(2):
        block = gathered_ref[:, :, 256 * part : 256 * part + 256].astype(jnp.float32)
        for parity in range(2):
            rows = block[:, 8 * parity : 8 * parity + 8].reshape(128, 256)
            spectrum[part, :, 128 * parity : 128 * parity + 128] = rows.T
    sums = jnp.sum(
        gathered_ref[:, :, 512:640].astype(jnp.float32).reshape(256, 128), axis=0, keepdims=True
    )
    norm_row = sums[:, :MASSES] + sums[:, MASSES:]
    lane_id = lax.broadcasted_iota(jnp.int32, (1, MASSES), 1)
    series[...] = jnp.zeros_like(series)

    def multiply(slot, place):
        for i in range(0, DFT_COLS, STRIP):
            here, there = slice(i, i + STRIP), slice(256 * place + i, 256 * place + i + STRIP)
            cosine, sine = waves_ref[slot, 0, here, :], waves_ref[slot, 1, here, :]
            re, im = spectrum[0, here, :], spectrum[1, here, :]
            real_part = (re * cosine - im * sine).astype(jnp.bfloat16)
            imag_part = (re * sine + im * cosine).astype(jnp.bfloat16)
            for parity in range(2):
                lanes = slice(128 * parity, 128 * parity + 128)
                products[parity, there, 0:128] = real_part[:, lanes]
                products[parity, there, 128:256] = imag_part[:, lanes]

    def twist(place):
        for i in range(0, DFT_COLS, STRIP):
            here, below = slice(i, i + STRIP), slice(256 + i, 256 + i + STRIP)
            there = slice(256 * place + i, 256 * place + i + STRIP)
            even_re, even_im = middle[0, there, 0:256], middle[0, there, 256:512]
            odd_re, odd_im = middle[1, there, 0:256], middle[1, there, 256:512]
            c, s = twist_ref[0, here, :], twist_ref[1, here, :]
            for side in range(2):
                lanes = slice(256 * side, 256 * side + 256)
                upper = even_re - odd_re if side else even_re + odd_re
                lower = even_im - odd_im if side else even_im + odd_im
                twisted[place, here, lanes] = (upper * c - lower * s).astype(jnp.bfloat16)
                twisted[place, below, lanes] = (upper * s + lower * c).astype(jnp.bfloat16)

    def finish(slot, place):
        mass = indices_ref[slot] % 64
        norm = jnp.sum(jnp.where(lane_id == mass, norm_row, 0.0), axis=1, keepdims=True)
        scale = lax.rsqrt(norm) * jnp.where(slot < count, 1.0, 0.0)
        for side in range(2):
            result = jnp.dot(
                last_ref[side],
                twisted[place, :, 256 * side : 256 * side + 256],
                preferred_element_type=jnp.float32,
            )
            scaled = result[: 2 * COLS] * scale
            for i in range(2):
                series[2 * side + i, pl.ds(slot, 2 * COLS, stride=TPL_DEV), :] = scaled[
                    :, 128 * i : 128 * i + 128
                ]

    @pl.loop(0, (count + BATCH - 1) // BATCH)
    def _(batch):
        for place in range(BATCH):
            multiply(batch * BATCH + place, place)
        for parity in range(2):
            middle[parity] = jnp.dot(
                products[parity], first_ref[parity], preferred_element_type=jnp.float32
            )
        for place in range(BATCH):
            twist(place)
        for place in range(BATCH):
            finish(batch * BATCH + place, place)

    def write(out_ref, half):
        for part in range(2):
            start = (part * COLS + 4 * half) * TPL_DEV
            for i in range(SPAN // 128):
                column, tile = divmod(i + 3, 4)
                rows = pl.ds(pl.multiple_of(start + column * TPL_DEV, TPL_DEV), TPL_DEV)
                out_ref[part, :, 128 * i : 128 * i + 128] = series[tile, rows, :].astype(
                    jnp.bfloat16
                )

    write(own_ref, half_ref[0])
    write(send_ref, 1 - half_ref[0])


def coherent_kernel(
    half_ref,
    delay_ref,
    near_gain_ref,
    far_gain_ref,
    own_ref,
    got_ref,
    out_ref,
    near,
    far,
    tiles,
    sems,
):
    def unpack(near_ref, far_ref):
        for part in range(2):
            near[part] = near_ref[part, :, 128 : 128 + HALF].astype(jnp.float32)
            far[part] = far_ref[part].astype(jnp.float32)[:, 64 : 64 + HALF + 128]

    @pl.when(half_ref[0] == 0)
    def _():
        unpack(own_ref, got_ref)

    @pl.when(half_ref[0] == 1)
    def _():
        unpack(got_ref, own_ref)

    lane_id = lax.broadcasted_iota(jnp.int32, (8, 128), 1)

    def copy_out(tile):
        lanes = pl.ds(pl.multiple_of(tile * 128, 128), 128)
        return pltpu.make_async_copy(tiles.at[tile], out_ref.at[:, lanes], sems.at[tile])

    @pl.loop(0, TILES // GROUP)
    def _(group):
        first_lane = pl.multiple_of(group * GROUP * 128, 128)
        for sky in range(SKY):
            shift = delay_ref[sky] + 64
            gain_near, gain_far = near_gain_ref[sky], far_gain_ref[sky]
            power = gain_near * gain_near + gain_far * gain_far
            inverse = lax.rsqrt(jnp.full((1, 128), power, jnp.float32))
            near_row = jnp.broadcast_to(gain_near * inverse, (8, 128))
            far_row = jnp.broadcast_to(gain_far * inverse, (8, 128))
            keep = lane_id < 128 - shift
            for upper in (0, 8):
                rows = slice(upper, upper + 8)
                total = [None] * GROUP
                for part in range(2):
                    rolled = [
                        pltpu.roll(far[part, rows, pl.ds(first_lane + 128 * i, 128)], 128 - shift, axis=1)
                        for i in range(GROUP + 1)
                    ]
                    for i in range(GROUP):
                        shifted = jnp.where(keep, rolled[i], rolled[i + 1])
                        own = near[part, rows, pl.ds(first_lane + 128 * i, 128)]
                        mixed = near_row * own + far_row * shifted
                        squared = mixed * mixed
                        total[i] = squared if part == 0 else total[i] + squared
                for i in range(GROUP):
                    place = pl.ds(sky + SKY * upper, 8, stride=SKY)
                    tiles[group * GROUP + i, place, :] = total[i]
        for i in range(GROUP):
            copy_out(group * GROUP + i).start()

    for tile in range(TILES):
        copy_out(tile).wait()


VMEM = pl.BlockSpec(memory_space=pltpu.VMEM)
SMEM = pl.BlockSpec(memory_space=pltpu.SMEM)


def on_device(strain, asd_inv, indices, counts, sky_delay, gain_near, gain_far):
    powers, first_tables, twist, last, scalars = constant_tables()
    z_groups, xy_groups = group_lists()
    bank = lax.axis_index("bank").astype(jnp.int32)[None]
    half = lax.axis_index("det").astype(jnp.int32)[None]
    payload = pl.pallas_call(
        prepare_kernel,
        out_shape=jax.ShapeDtypeStruct((N_Z, 1, PAYLOAD), jnp.float32),
        in_specs=[SMEM, VMEM, VMEM],
        out_specs=VMEM,
    )(bank, strain[0], asd_inv)
    line = lax.all_to_all(payload, "bank", 0, 0, axis_index_groups=z_groups)
    spread = pl.pallas_call(
        spread_kernel,
        out_shape=jax.ShapeDtypeStruct((N_XY, N_Z, PAYLOAD), jnp.bfloat16),
        in_specs=[VMEM],
        out_specs=VMEM,
    )(line)
    plane = lax.all_to_all(spread, "bank", 0, 0, axis_index_groups=xy_groups)
    waves = pl.pallas_call(
        wave_kernel,
        out_shape=jax.ShapeDtypeStruct((TPL_DEV, 2, DFT_COLS, 256), jnp.float32),
        in_specs=[SMEM] * 3 + [VMEM],
        out_specs=VMEM,
        cost_estimate=pl.CostEstimate(flops=40 * 2**20, bytes_accessed=10 * 2**20, transcendentals=2**20),
        compiler_params=pltpu.CompilerParams(vmem_limit_bytes=16 * 1024 * 1024),
    )(indices, counts, scalars, powers)
    window = jax.ShapeDtypeStruct((2, TPL_DEV, SPAN), jnp.bfloat16)
    own, send = pl.pallas_call(
        filter_kernel,
        out_shape=(window, window),
        in_specs=[SMEM] * 3 + [VMEM] * 5,
        out_specs=(VMEM, VMEM),
        scratch_shapes=[
            pltpu.VMEM((2, DFT_COLS, 256), jnp.float32),
            pltpu.VMEM((2, BATCH * DFT_COLS, 256), jnp.bfloat16),
            pltpu.VMEM((2, BATCH * DFT_COLS, 512), jnp.float32),
            pltpu.VMEM((BATCH, 512, 512), jnp.bfloat16),
            pltpu.VMEM((4, 2 * COLS * TPL_DEV, 128), jnp.float32),
        ],
        compiler_params=pltpu.CompilerParams(vmem_limit_bytes=24 * 1024 * 1024),
    )(indices, counts, half, waves, plane, first_tables, twist, last)
    got = lax.ppermute(send, "det", [(0, 1), (1, 0)])
    out = pl.pallas_call(
        coherent_kernel,
        out_shape=jax.ShapeDtypeStruct((TPL_DEV * SKY, HALF), jnp.float32),
        in_specs=[SMEM] * 4 + [VMEM] * 2,
        out_specs=pl.BlockSpec(memory_space=pl.ANY),
        scratch_shapes=[
            pltpu.VMEM((2, TPL_DEV, HALF), jnp.float32),
            pltpu.VMEM((2, TPL_DEV, HALF + 128), jnp.float32),
            pltpu.VMEM((TILES, TPL_DEV * SKY, 128), jnp.float32),
            pltpu.SemaphoreType.DMA((TILES,)),
        ],
        compiler_params=pltpu.CompilerParams(vmem_limit_bytes=16 * 1024 * 1024),
    )(half, sky_delay, gain_near, gain_far, own, got)
    return out.reshape(TPL_DEV, SKY, HALF)


def solution(mesh):
    return jax.shard_map(
        on_device,
        mesh=mesh,
        in_specs=(P("det", None, "bank"), P("det", "bank"), P("bank"), P("bank"), P(), P(), P()),
        out_specs=P("bank", None, "det"),
        check_vma=False,
    )
```

```python
import functools
import math

import jax
import jax.numpy as jnp
import numpy as np
from jax import lax
from jax.experimental import pallas as pl
from jax.experimental.pallas import tpu as pltpu
from jax.sharding import PartitionSpec as P

DFT_ROWS = 512
DFT_COLS = 256
SAMPLES = 131072
LOW_BIN = 1920
WIN_BLOCKS = 8
WINDOW = 4096
HALF = WINDOW // 2
TPL_DEV = 16
SKY = 16
MASSES = 64
N_Z = 16
N_XY = 16
COLS = WIN_BLOCKS + 2
SPAN = HALF + 256
PAYLOAD = 640
STRIP = 16
BATCH = 4
STORED = 3
TILES = HALF // 128
GROUP = 4
STAGES = 4
BIG = 60 * 1024 * 1024
FILTER_VMEM = 46 * 1024 * 1024
WAVE_ROOM = 80

MSUN_SEC = 4.925491e-06
SAMPLE_RATE = 2048.0

Z_ORDER = [8, 10, 12, 14, 0, 2, 4, 6, 9, 11, 13, 15, 1, 3, 5, 7]
XY_ORDER = [(k + 5) % N_XY for k in range(N_XY)]


def group_lists():
    z_groups = [[q * N_Z + z for z in Z_ORDER] for q in range(N_XY)]
    xy_groups = [[q * N_Z + z for q in XY_ORDER] for z in range(N_Z)]
    return z_groups, xy_groups


def constant_tables():
    rows = np.array([[q * N_Z + z for z in Z_ORDER] for q in XY_ORDER])
    even, odd = rows[:, :8].reshape(-1), rows[:, 8:].reshape(-1)
    k1 = np.concatenate([even, odd])
    k2 = np.arange(DFT_COLS)
    bins = 256 * k1[None, :] + k2[:, None]
    freq = np.maximum(bins * (SAMPLE_RATE / SAMPLES), 1.0)
    powers = np.stack(
        [
            freq ** (-5.0 / 3.0),
            freq**-1.0,
            freq ** (-2.0 / 3.0),
            np.where(bins >= LOW_BIN, freq ** (-7.0 / 6.0), 0.0),
            freq**4,
        ]
    ).astype(np.float32)

    t1 = np.arange(256)

    def first(rows_k):
        angle = 2.0 * np.pi / 512 * (rows_k[:, None] * t1[None, :] % 512)
        c, s = np.cos(angle), np.sin(angle)
        return np.concatenate([np.concatenate([c, s], 1), np.concatenate([-s, c], 1)], 0)

    first_tables = np.stack([first(even), first(odd)])
    angle = 2.0 * np.pi / SAMPLES * (k2[:, None] * t1[None, :] % SAMPLES)
    twist = np.stack([np.cos(angle), np.sin(angle)]).astype(np.float32)
    t2 = DFT_COLS // 2 - WIN_BLOCKS // 2 - 1 + np.arange(COLS)
    last = np.zeros((2, 32, 512))
    for side in range(2):
        steps = k2[None, :] * (t2[:, None] * DFT_ROWS + 256 * side)
        angle = 2.0 * np.pi / SAMPLES * (steps % SAMPLES)
        c, s = np.cos(angle), np.sin(angle)
        last[side, :COLS] = np.concatenate([c, -s], 1)
        last[side, COLS : 2 * COLS] = np.concatenate([s, c], 1)

    seconds = 6.0 * 1.03 ** np.arange(MASSES) * MSUN_SEC
    ratio = 0.16 + 0.09 * np.arange(64) / 63.0
    x = np.pi * seconds
    turn = 1.0 / (2.0 * np.pi)
    scalars = np.stack(
        [
            turn * x ** (-5.0 / 3.0),
            turn * x**-1.0,
            turn * x ** (-2.0 / 3.0),
            -((6.0**1.5 * x) ** 4) / math.log(2.0),
            3.0 / (128.0 * ratio),
            3715.0 / 756.0 + 55.0 * ratio / 9.0,
            (113.0 - 76.0 * ratio) / 12.0,
            np.zeros(64),
        ]
    ).astype(np.float32)
    return (
        powers,
        first_tables.astype(jnp.bfloat16),
        twist,
        last.astype(jnp.bfloat16),
        scalars,
    )


def even_fit(function, terms):
    nodes = 0.5 * np.cos(np.pi * (np.arange(400) + 0.5) / 400)
    design = (nodes[:, None] ** 2) ** np.arange(terms)[None, :]
    fitted = np.linalg.lstsq(design, function(nodes), rcond=None)[0]
    return [float(np.float32(v)) for v in fitted]


ROOT2 = math.sqrt(2.0)
SIN_FIT = even_fit(lambda r: ROOT2 * np.pi * np.sinc(r), 5)
COS_FIT = even_fit(lambda r: ROOT2 * np.cos(np.pi * r), 5)
ROUND_SHIFT = 12582912.0


def horner(coefs, square):
    total = coefs[-1] * square + coefs[-2]
    for c in coefs[-3::-1]:
        total = total * square + c
    return total


def payload_row(bank, strain, asd):
    weight = asd * asd
    over = (strain * weight).astype(jnp.bfloat16).astype(jnp.float32)
    bin_id = bank * 256 + lax.broadcasted_iota(jnp.int32, (1, 256), 1)
    clipped = jnp.maximum(bin_id.astype(jnp.float32) * (SAMPLE_RATE / SAMPLES), 1.0)
    square = clipped * clipped
    falling = jnp.exp((-7.0 / 3.0) * jnp.log(clipped))
    weighted = jnp.where(bin_id >= LOW_BIN, falling, 0.0) * weight
    mass_id = lax.broadcasted_iota(jnp.int32, (MASSES, 1), 0).astype(jnp.float32)
    start = math.log(2.0) + 4.0 * math.log(6.0**1.5 * math.pi * 6.0 * MSUN_SEC)
    steep = jnp.exp(4.0 * math.log(1.03) * mass_id + start)
    column = jnp.sum(jnp.exp(-steep * (square * square)) * weighted, axis=1, keepdims=True)
    row_id = lax.broadcasted_iota(jnp.int32, (MASSES, MASSES), 0)
    col_id = lax.broadcasted_iota(jnp.int32, (MASSES, MASSES), 1)
    norms = jnp.sum(jnp.where(row_id == col_id, column, 0.0), axis=0, keepdims=True)
    coarse = norms.astype(jnp.bfloat16).astype(jnp.float32)
    return jnp.concatenate([over[0:1], over[1:2], coarse, norms - coarse], axis=1)


def slot_scalars(slot, indices_ref, scalars_ref):
    entry = indices_ref[slot]
    mass, eta = entry % 64, entry // 64 % 64
    spin = -0.6 + 0.4 * (entry // 4096).astype(jnp.float32)
    lead = scalars_ref[4, eta]
    c53 = lead * scalars_ref[0, mass]
    c1 = lead * scalars_ref[5, eta] * scalars_ref[1, mass]
    c23 = lead * (4.0 * spin * scalars_ref[6, eta] - 16.0 * math.pi) * scalars_ref[2, mass]
    return c53, c1, c23, scalars_ref[3, mass]


def wave(coefs, powers, here):
    c53, c1, c23, steep = coefs
    turns = (
        c53 * powers[0, here, :] + c1 * powers[1, here, :] + (c23 * powers[2, here, :] - 0.125)
    )
    rest = turns - ((turns + ROUND_SHIFT) - ROUND_SHIFT)
    square = rest * rest
    half_sin = horner(SIN_FIT, square) * rest
    half_cos = horner(COS_FIT, square)
    envelope = powers[3, here, :] * jnp.exp2(steep * powers[4, here, :])
    return envelope * (1.0 - half_sin * half_sin), envelope * (half_sin * half_cos)


def wave_kernel(indices_ref, counts_ref, scalars_ref, powers_hbm, waves_ref, powers, staged, sems):
    steps = rounded_up(counts_ref[0]) // BATCH * STORED

    def store(step):
        place = step % STAGES
        return pltpu.make_async_copy(staged.at[place], waves_ref.at[step], sems.at[place])

    def load(strip):
        rows = pl.ds(strip * 64, 64)
        return pltpu.make_async_copy(
            powers_hbm.at[:, rows], powers.at[:, rows], sems.at[STAGES + strip]
        )

    for strip in range(4):
        load(strip).start()

    @pl.loop(0, steps)
    def _(step):
        slot = step // STORED * BATCH + step % STORED
        coefs = slot_scalars(slot, indices_ref, scalars_ref)

        @pl.when(step >= STAGES)
        def _():
            store(step - STAGES).wait()

        @pl.loop(0, DFT_COLS // 64)
        def _(strip):
            @pl.when(step == 0)
            def _():
                load(strip).wait()

            for piece in range(4):
                here = pl.ds(pl.multiple_of(strip * 64 + piece * 16, 16), 16)
                cosine, sine = wave(coefs, powers, here)
                staged[step % STAGES, 0, here, :] = cosine.astype(jnp.bfloat16)
                staged[step % STAGES, 1, here, :] = sine.astype(jnp.bfloat16)

        store(step).start()

    for back in range(STAGES, 0, -1):

        @pl.when(steps >= back)
        def _():
            store(steps - back).wait()


def rounded_up(count):
    return (count + BATCH - 1) // BATCH * BATCH


def prepare_kernel(bank_ref, strain_ref, asd_ref, out_ref):
    row = payload_row(bank_ref[0], strain_ref[...], asd_ref[...])
    out_ref[...] = jnp.broadcast_to(row[:, None, :], (N_Z, 1, PAYLOAD))


def spread_kernel(line_ref, out_ref):
    line = line_ref[...].reshape(N_Z, PAYLOAD).astype(jnp.bfloat16)
    for i in range(N_XY):
        out_ref[i] = line


def filter_kernel(
    indices_ref,
    counts_ref,
    half_ref,
    scalars_ref,
    gathered_ref,
    first_ref,
    twist_ref,
    last_ref,
    powers_ref,
    waves_ref,
    own_ref,
    send_ref,
    spectrum,
    products,
    middle,
    twisted,
    series,
    waves,
    sems,
):
    count = counts_ref[0]
    batches = rounded_up(count) // BATCH
    steps = batches * STORED

    def fetch(step):
        place = step % (2 * STORED)
        return pltpu.make_async_copy(waves_ref.at[step], waves.at[place], sems.at[place])

    @pl.loop(0, jnp.minimum(steps, 2 * STORED))
    def _(step):
        fetch(step).start()

    for part in range(2):
        block = gathered_ref[:, :, 256 * part : 256 * part + 256].astype(jnp.float32)
        for parity in range(2):
            rows = block[:, 8 * parity : 8 * parity + 8].reshape(128, 256)
            spectrum[part, :, 128 * parity : 128 * parity + 128] = rows.T
    sums = jnp.sum(
        gathered_ref[:, :, 512:640].astype(jnp.float32).reshape(256, 128), axis=0, keepdims=True
    )
    norm_row = sums[:, :MASSES] + sums[:, MASSES:]
    lane_id = lax.broadcasted_iota(jnp.int32, (1, MASSES), 1)
    series[...] = jnp.zeros_like(series)

    def multiply(batch, place):
        if place < STORED:
            step = batch * STORED + place
            buffer = step % (2 * STORED)
            fetch(step).wait()
        else:
            coefs = slot_scalars(batch * BATCH + place, indices_ref, scalars_ref)
        for i in range(0, DFT_COLS, STRIP):
            here, there = slice(i, i + STRIP), slice(256 * place + i, 256 * place + i + STRIP)
            if place < STORED:
                cosine = waves[buffer, 0, here, :].astype(jnp.float32)
                sine = waves[buffer, 1, here, :].astype(jnp.float32)
            else:
                cosine, sine = wave(coefs, powers_ref, here)
            re, im = spectrum[0, here, :], spectrum[1, here, :]
            real_part = (re * cosine - im * sine).astype(jnp.bfloat16)
            imag_part = (re * sine + im * cosine).astype(jnp.bfloat16)
            for parity in range(2):
                lanes = slice(128 * parity, 128 * parity + 128)
                products[parity, there, 0:128] = real_part[:, lanes]
                products[parity, there, 128:256] = imag_part[:, lanes]

    def twist(place):
        for i in range(0, DFT_COLS, STRIP):
            here, below = slice(i, i + STRIP), slice(256 + i, 256 + i + STRIP)
            there = slice(256 * place + i, 256 * place + i + STRIP)
            even_re, even_im = middle[0, there, 0:256], middle[0, there, 256:512]
            odd_re, odd_im = middle[1, there, 0:256], middle[1, there, 256:512]
            c, s = twist_ref[0, here, :], twist_ref[1, here, :]
            for side in range(2):
                lanes = slice(256 * side, 256 * side + 256)
                upper = even_re - odd_re if side else even_re + odd_re
                lower = even_im - odd_im if side else even_im + odd_im
                twisted[place, here, lanes] = (upper * c - lower * s).astype(jnp.bfloat16)
                twisted[place, below, lanes] = (upper * s + lower * c).astype(jnp.bfloat16)

    def finish(slot, place):
        mass = indices_ref[slot] % 64
        norm = jnp.sum(jnp.where(lane_id == mass, norm_row, 0.0), axis=1, keepdims=True)
        scale = lax.rsqrt(norm) * jnp.where(slot < count, 1.0, 0.0)
        for side in range(2):
            result = jnp.dot(
                last_ref[side],
                twisted[place, :, 256 * side : 256 * side + 256],
                preferred_element_type=jnp.float32,
            )
            scaled = result[: 2 * COLS] * scale
            for i in range(2):
                series[2 * side + i, pl.ds(slot, 2 * COLS, stride=TPL_DEV), :] = scaled[
                    :, 128 * i : 128 * i + 128
                ]

    @pl.loop(0, batches)
    def _(batch):
        for place in range(BATCH):
            multiply(batch, place)

        for place in range(STORED):
            later = (batch + 2) * STORED + place

            @pl.when(later < steps)
            def _():
                fetch(later).start()

        for parity in range(2):
            middle[parity] = jnp.dot(
                products[parity], first_ref[parity], preferred_element_type=jnp.float32
            )
        for place in range(BATCH):
            twist(place)
        for place in range(BATCH):
            finish(batch * BATCH + place, place)

    def write(out_ref, half):
        for part in range(2):
            start = (part * COLS + 4 * half) * TPL_DEV
            for i in range(SPAN // 128):
                column, tile = divmod(i + 3, 4)
                rows = pl.ds(pl.multiple_of(start + column * TPL_DEV, TPL_DEV), TPL_DEV)
                out_ref[part, :, 128 * i : 128 * i + 128] = series[tile, rows, :].astype(
                    jnp.bfloat16
                )

    write(own_ref, half_ref[0])
    write(send_ref, 1 - half_ref[0])


def coherent_kernel(
    half_ref,
    delay_ref,
    near_gain_ref,
    far_gain_ref,
    own_ref,
    got_ref,
    out_ref,
    near,
    far,
    tiles,
    sems,
):
    def unpack(near_ref, far_ref):
        for part in range(2):
            near[part] = near_ref[part, :, 128 : 128 + HALF].astype(jnp.float32)
            far[part] = far_ref[part].astype(jnp.float32)[:, 64 : 64 + HALF + 128]

    @pl.when(half_ref[0] == 0)
    def _():
        unpack(own_ref, got_ref)

    @pl.when(half_ref[0] == 1)
    def _():
        unpack(got_ref, own_ref)

    lane_id = lax.broadcasted_iota(jnp.int32, (8, 128), 1)

    def copy_out(tile):
        lanes = pl.ds(pl.multiple_of(tile * 128, 128), 128)
        return pltpu.make_async_copy(tiles.at[tile], out_ref.at[:, lanes], sems.at[tile])

    @pl.loop(0, TILES // GROUP)
    def _(group):
        first_lane = pl.multiple_of(group * GROUP * 128, 128)
        for sky in range(SKY):
            shift = delay_ref[sky] + 64
            gain_near, gain_far = near_gain_ref[sky], far_gain_ref[sky]
            power = gain_near * gain_near + gain_far * gain_far
            inverse = lax.rsqrt(jnp.full((1, 128), power, jnp.float32))
            near_row = jnp.broadcast_to(gain_near * inverse, (8, 128))
            far_row = jnp.broadcast_to(gain_far * inverse, (8, 128))
            keep = lane_id < 128 - shift
            for upper in (0, 8):
                rows = slice(upper, upper + 8)
                total = [None] * GROUP
                for part in range(2):
                    rolled = [
                        pltpu.roll(far[part, rows, pl.ds(first_lane + 128 * i, 128)], 128 - shift, axis=1)
                        for i in range(GROUP + 1)
                    ]
                    for i in range(GROUP):
                        shifted = jnp.where(keep, rolled[i], rolled[i + 1])
                        own = near[part, rows, pl.ds(first_lane + 128 * i, 128)]
                        mixed = near_row * own + far_row * shifted
                        squared = mixed * mixed
                        total[i] = squared if part == 0 else total[i] + squared
                for i in range(GROUP):
                    place = pl.ds(sky + SKY * upper, 8, stride=SKY)
                    tiles[group * GROUP + i, place, :] = total[i]
        for i in range(GROUP):
            copy_out(group * GROUP + i).start()

    for tile in range(TILES):
        copy_out(tile).wait()


ANY = pl.BlockSpec(memory_space=pl.ANY)
VMEM = pl.BlockSpec(memory_space=pltpu.VMEM)
SMEM = pl.BlockSpec(memory_space=pltpu.SMEM)


def on_device(strain, asd_inv, indices, counts, sky_delay, gain_near, gain_far):
    powers, first_tables, twist, last, scalars = constant_tables()
    z_groups, xy_groups = group_lists()
    bank = lax.axis_index("bank").astype(jnp.int32)[None]
    half = lax.axis_index("det").astype(jnp.int32)[None]
    payload = pl.pallas_call(
        prepare_kernel,
        out_shape=jax.ShapeDtypeStruct((N_Z, 1, PAYLOAD), jnp.float32),
        in_specs=[SMEM, VMEM, VMEM],
        out_specs=VMEM,
        compiler_params=pltpu.CompilerParams(vmem_limit_bytes=BIG),
    )(bank, strain[0], asd_inv)
    line = lax.all_to_all(payload, "bank", 0, 0, axis_index_groups=z_groups)
    spread = pl.pallas_call(
        spread_kernel,
        out_shape=jax.ShapeDtypeStruct((N_XY, N_Z, PAYLOAD), jnp.bfloat16),
        in_specs=[VMEM],
        out_specs=VMEM,
    )(line)
    plane = lax.all_to_all(spread, "bank", 0, 0, axis_index_groups=xy_groups)
    waves = pl.pallas_call(
        wave_kernel,
        out_shape=jax.ShapeDtypeStruct((WAVE_ROOM, 2, DFT_COLS, 256), jnp.bfloat16),
        in_specs=[SMEM] * 3 + [ANY],
        out_specs=ANY,
        scratch_shapes=[
            pltpu.VMEM((5, DFT_COLS, 256), jnp.float32),
            pltpu.VMEM((STAGES, 2, DFT_COLS, 256), jnp.bfloat16),
            pltpu.SemaphoreType.DMA((STAGES + 4,)),
        ],
        cost_estimate=pl.CostEstimate(
            flops=40 * 2**20, bytes_accessed=10 * 2**20, transcendentals=2**20
        ),
        compiler_params=pltpu.CompilerParams(vmem_limit_bytes=BIG),
    )(indices, counts, scalars, powers)
    window = jax.ShapeDtypeStruct((2, TPL_DEV, SPAN), jnp.bfloat16)
    own, send = pl.pallas_call(
        filter_kernel,
        out_shape=(window, window),
        in_specs=[SMEM] * 4 + [VMEM] * 5 + [ANY],
        out_specs=(VMEM, VMEM),
        scratch_shapes=[
            pltpu.VMEM((2, DFT_COLS, 256), jnp.float32),
            pltpu.VMEM((2, BATCH * DFT_COLS, 256), jnp.bfloat16),
            pltpu.VMEM((2, BATCH * DFT_COLS, 512), jnp.float32),
            pltpu.VMEM((BATCH, 512, 512), jnp.bfloat16),
            pltpu.VMEM((4, 2 * COLS * TPL_DEV, 128), jnp.float32),
            pltpu.VMEM((2 * STORED, 2, DFT_COLS, 256), jnp.bfloat16),
            pltpu.SemaphoreType.DMA((2 * STORED,)),
        ],
        compiler_params=pltpu.CompilerParams(vmem_limit_bytes=FILTER_VMEM),
    )(indices, counts, half, scalars, plane, first_tables, twist, last, powers, waves)
    got = lax.ppermute(send, "det", [(0, 1), (1, 0)])
    out = pl.pallas_call(
        coherent_kernel,
        out_shape=jax.ShapeDtypeStruct((TPL_DEV * SKY, HALF), jnp.float32),
        in_specs=[SMEM] * 4 + [VMEM] * 2,
        out_specs=pl.BlockSpec(memory_space=pl.ANY),
        scratch_shapes=[
            pltpu.VMEM((2, TPL_DEV, HALF), jnp.float32),
            pltpu.VMEM((2, TPL_DEV, HALF + 128), jnp.float32),
            pltpu.VMEM((TILES, TPL_DEV * SKY, 128), jnp.float32),
            pltpu.SemaphoreType.DMA((TILES,)),
        ],
        compiler_params=pltpu.CompilerParams(vmem_limit_bytes=16 * 1024 * 1024),
    )(half, sky_delay, gain_near, gain_far, own, got)
    return out.reshape(TPL_DEV, SKY, HALF)


def solution(mesh):
    return jax.shard_map(
        on_device,
        mesh=mesh,
        in_specs=(P("det", None, "bank"), P("det", "bank"), P("bank"), P("bank"), P(), P(), P()),
        out_specs=P("bank", None, "det"),
        check_vma=False,
    )
```

```python
import functools
import math

import jax
import jax.numpy as jnp
import numpy as np
from jax import lax
from jax.experimental import pallas as pl
from jax.experimental.pallas import tpu as pltpu
from jax.sharding import PartitionSpec as P

DFT_ROWS = 512
DFT_COLS = 256
SAMPLES = 131072
LOW_BIN = 1920
WIN_BLOCKS = 8
WINDOW = 4096
HALF = WINDOW // 2
TPL_DEV = 16
SKY = 16
MASSES = 64
N_Z = 16
N_XY = 16
COLS = WIN_BLOCKS + 2
SPAN = HALF + 128
PAYLOAD = 640
STRIP = 16
BATCH = 4
STORED = 3
INLINE = BATCH - STORED
TILES = HALF // 128
GROUP = 8
STAGES = 4
BIG = 60 * 1024 * 1024
FILTER_VMEM = 46 * 1024 * 1024
WAVE_ROOM = 80

MSUN_SEC = 4.925491e-06
SAMPLE_RATE = 2048.0

Z_ORDER = [9, 11, 13, 15, 1, 3, 5, 7, 8, 10, 12, 14, 0, 2, 4, 6]
XY_ORDER = [(k + 5) % N_XY for k in range(N_XY)]


def group_lists():
    z_groups = [[q * N_Z + z for z in Z_ORDER] for q in range(N_XY)]
    xy_groups = [[q * N_Z + z for q in XY_ORDER] for z in range(N_Z)]
    return z_groups, xy_groups


def constant_tables():
    rows = np.array([[q * N_Z + z for z in Z_ORDER] for q in XY_ORDER])
    odd, even = rows[:, :8].reshape(-1), rows[:, 8:].reshape(-1)
    k1 = np.concatenate([odd, even])
    k2 = np.arange(DFT_COLS)
    bins = 256 * k1[None, :] + k2[:, None]
    freq = np.maximum(bins * (SAMPLE_RATE / SAMPLES), 1.0)
    powers = np.stack(
        [
            freq ** (-5.0 / 3.0),
            freq**-1.0,
            freq ** (-2.0 / 3.0),
            np.where(bins >= LOW_BIN, freq ** (-7.0 / 6.0), 0.0),
            freq**4,
        ]
    ).astype(np.float32)

    t1 = np.arange(256)

    def first(rows_k):
        angle = 2.0 * np.pi / 512 * (rows_k[:, None] * t1[None, :] % 512)
        c, s = np.cos(angle), np.sin(angle)
        return np.concatenate([np.concatenate([c, s], 1), np.concatenate([-s, c], 1)], 0)

    first_tables = np.stack([first(odd), first(even)])
    angle = 2.0 * np.pi / SAMPLES * (k2[:, None] * t1[None, :] % SAMPLES)
    twist = np.stack([np.cos(angle), np.sin(angle)]).astype(np.float32)
    t2 = DFT_COLS // 2 - WIN_BLOCKS // 2 - 1 + np.arange(COLS)
    last = np.zeros((2, 32, 512))
    for side in range(2):
        steps = k2[None, :] * (t2[:, None] * DFT_ROWS + 256 * side)
        angle = 2.0 * np.pi / SAMPLES * (steps % SAMPLES)
        c, s = np.cos(angle), np.sin(angle)
        last[side, :COLS] = np.concatenate([c, -s], 1)
        last[side, COLS : 2 * COLS] = np.concatenate([s, c], 1)

    seconds = 6.0 * 1.03 ** np.arange(MASSES) * MSUN_SEC
    ratio = 0.16 + 0.09 * np.arange(64) / 63.0
    x = np.pi * seconds
    turn = 1.0 / (2.0 * np.pi)
    scalars = np.stack(
        [
            turn * x ** (-5.0 / 3.0),
            turn * x**-1.0,
            turn * x ** (-2.0 / 3.0),
            -((6.0**1.5 * x) ** 4) / math.log(2.0),
            3.0 / (128.0 * ratio),
            3715.0 / 756.0 + 55.0 * ratio / 9.0,
            (113.0 - 76.0 * ratio) / 12.0,
            np.zeros(64),
        ]
    ).astype(np.float32)
    return (
        powers,
        first_tables.astype(jnp.bfloat16),
        twist,
        last.astype(jnp.bfloat16),
        scalars,
    )


def even_fit(function, terms):
    nodes = 0.5 * np.cos(np.pi * (np.arange(400) + 0.5) / 400)
    design = (nodes[:, None] ** 2) ** np.arange(terms)[None, :]
    fitted = np.linalg.lstsq(design, function(nodes), rcond=None)[0]
    return [float(np.float32(v)) for v in fitted]


ROOT2 = math.sqrt(2.0)
SIN_FIT = even_fit(lambda r: ROOT2 * np.pi * np.sinc(r), 5)
ROUND_SHIFT = 12582912.0


def horner(coefs, square):
    total = coefs[-1] * square + coefs[-2]
    for c in coefs[-3::-1]:
        total = total * square + c
    return total


def payload_row(bank, strain, asd):
    weight = asd * asd
    over = (strain * weight).astype(jnp.bfloat16).astype(jnp.float32)
    bin_id = bank * 256 + lax.broadcasted_iota(jnp.int32, (1, 256), 1)
    clipped = jnp.maximum(bin_id.astype(jnp.float32) * (SAMPLE_RATE / SAMPLES), 1.0)
    square = clipped * clipped
    falling = jnp.exp((-7.0 / 3.0) * jnp.log(clipped))
    weighted = jnp.where(bin_id >= LOW_BIN, falling, 0.0) * weight
    mass_id = lax.broadcasted_iota(jnp.int32, (MASSES, 1), 0).astype(jnp.float32)
    start = math.log(2.0) + 4.0 * math.log(6.0**1.5 * math.pi * 6.0 * MSUN_SEC)
    steep = jnp.exp(4.0 * math.log(1.03) * mass_id + start)
    column = jnp.sum(jnp.exp(-steep * (square * square)) * weighted, axis=1, keepdims=True)
    row_id = lax.broadcasted_iota(jnp.int32, (MASSES, MASSES), 0)
    col_id = lax.broadcasted_iota(jnp.int32, (MASSES, MASSES), 1)
    norms = jnp.sum(jnp.where(row_id == col_id, column, 0.0), axis=0, keepdims=True)
    coarse = norms.astype(jnp.bfloat16).astype(jnp.float32)
    return jnp.concatenate([over[0:1], over[1:2], coarse, norms - coarse], axis=1)


def slot_scalars(slot, indices_ref, scalars_ref):
    entry = indices_ref[slot]
    mass, eta = entry % 64, entry // 64 % 64
    spin = -0.6 + 0.4 * (entry // 4096).astype(jnp.float32)
    lead = scalars_ref[4, eta]
    c53 = lead * scalars_ref[0, mass]
    c1 = lead * scalars_ref[5, eta] * scalars_ref[1, mass]
    c23 = lead * (4.0 * spin * scalars_ref[6, eta] - 16.0 * math.pi) * scalars_ref[2, mass]
    return c53, c1, c23, scalars_ref[3, mass]


def wave(coefs, powers, here):
    c53, c1, c23, steep = coefs
    turns = (
        c53 * powers[0, here, :] + c1 * powers[1, here, :] + (c23 * powers[2, here, :] - 0.125)
    )
    rest = turns - ((turns + ROUND_SHIFT) - ROUND_SHIFT)
    square = rest * rest
    half_sin = horner(SIN_FIT, square) * rest
    cosine = 1.0 - half_sin * half_sin
    above = jnp.maximum(1.0 + cosine, 1e-12)
    half_cos = above * lax.rsqrt(above)
    envelope = powers[3, here, :] * jnp.exp2(steep * powers[4, here, :])
    return envelope * cosine, envelope * (half_sin * half_cos)


def wave_kernel(indices_ref, counts_ref, scalars_ref, powers_hbm, waves_ref, powers, staged, sems):
    steps = rounded_up(counts_ref[0]) // BATCH * STORED

    def store(step):
        place = step % STAGES
        return pltpu.make_async_copy(staged.at[place], waves_ref.at[step], sems.at[place])

    def load(strip):
        rows = pl.ds(strip * 64, 64)
        return pltpu.make_async_copy(
            powers_hbm.at[:, rows], powers.at[:, rows], sems.at[STAGES + strip]
        )

    for strip in range(4):
        load(strip).start()

    @pl.loop(0, steps)
    def _(step):
        slot = step // STORED * BATCH + INLINE + step % STORED
        coefs = slot_scalars(slot, indices_ref, scalars_ref)

        @pl.when(step >= STAGES)
        def _():
            store(step - STAGES).wait()

        @pl.loop(0, DFT_COLS // 64)
        def _(strip):
            @pl.when(step == 0)
            def _():
                load(strip).wait()

            for piece in range(4):
                here = pl.ds(pl.multiple_of(strip * 64 + piece * 16, 16), 16)
                cosine, sine = wave(coefs, powers, here)
                staged[step % STAGES, 0, here, :] = cosine.astype(jnp.bfloat16)
                staged[step % STAGES, 1, here, :] = sine.astype(jnp.bfloat16)

        store(step).start()

    for back in range(STAGES, 0, -1):

        @pl.when(steps >= back)
        def _():
            store(steps - back).wait()


def rounded_up(count):
    return (count + BATCH - 1) // BATCH * BATCH


def prepare_kernel(bank_ref, strain_ref, asd_ref, out_ref):
    row = payload_row(bank_ref[0], strain_ref[...], asd_ref[...])
    out_ref[...] = jnp.broadcast_to(row[:, None, :], (N_Z, 1, PAYLOAD))


def spread_kernel(line_ref, out_ref):
    line = line_ref[...].reshape(N_Z, PAYLOAD).astype(jnp.bfloat16)
    for i in range(N_XY):
        out_ref[i] = line


def filter_kernel(
    indices_ref,
    counts_ref,
    half_ref,
    scalars_ref,
    gathered_ref,
    first_ref,
    twist_ref,
    last_ref,
    powers_ref,
    waves_ref,
    own_ref,
    send_ref,
    spectrum,
    products,
    middle,
    twisted,
    series,
    waves,
    sems,
):
    count = counts_ref[0]
    batches = rounded_up(count) // BATCH
    steps = batches * STORED

    def fetch(step):
        place = step % (2 * STORED)
        return pltpu.make_async_copy(waves_ref.at[step], waves.at[place], sems.at[place])

    @pl.loop(0, jnp.minimum(steps, 2 * STORED))
    def _(step):
        fetch(step).start()

    for part in range(2):
        block = gathered_ref[:, :, 256 * part : 256 * part + 256].astype(jnp.float32)
        for parity in range(2):
            rows = block[:, 8 * parity : 8 * parity + 8].reshape(128, 256)
            spectrum[part, :, 128 * parity : 128 * parity + 128] = rows.T
    sums = jnp.sum(
        gathered_ref[:, :, 512:640].astype(jnp.float32).reshape(256, 128), axis=0, keepdims=True
    )
    norm_row = sums[:, :MASSES] + sums[:, MASSES:]
    lane_id = lax.broadcasted_iota(jnp.int32, (1, MASSES), 1)
    series[...] = jnp.zeros_like(series)

    def multiply(batch, place):
        if place >= INLINE:
            step = batch * STORED + place - INLINE
            buffer = step % (2 * STORED)
            fetch(step).wait()
        else:
            coefs = slot_scalars(batch * BATCH + place, indices_ref, scalars_ref)
        for i in range(0, DFT_COLS, STRIP):
            here, there = slice(i, i + STRIP), slice(256 * place + i, 256 * place + i + STRIP)
            if place >= INLINE:
                cosine = waves[buffer, 0, here, :].astype(jnp.float32)
                sine = waves[buffer, 1, here, :].astype(jnp.float32)
            else:
                cosine, sine = wave(coefs, powers_ref, here)
            re, im = spectrum[0, here, :], spectrum[1, here, :]
            real_part = (re * cosine - im * sine).astype(jnp.bfloat16)
            imag_part = (re * sine + im * cosine).astype(jnp.bfloat16)
            for parity in range(2):
                lanes = slice(128 * parity, 128 * parity + 128)
                products[parity, there, 0:128] = real_part[:, lanes]
                products[parity, there, 128:256] = imag_part[:, lanes]

    def twist(place):
        for i in range(0, DFT_COLS, STRIP):
            here, below = slice(i, i + STRIP), slice(256 + i, 256 + i + STRIP)
            there = slice(256 * place + i, 256 * place + i + STRIP)
            odd_re, odd_im = middle[0, there, 0:256], middle[0, there, 256:512]
            even_re, even_im = middle[1, there, 0:256], middle[1, there, 256:512]
            c, s = twist_ref[0, here, :], twist_ref[1, here, :]
            for side in range(2):
                lanes = slice(256 * side, 256 * side + 256)
                upper = even_re - odd_re if side else even_re + odd_re
                lower = even_im - odd_im if side else even_im + odd_im
                twisted[place, here, lanes] = (upper * c - lower * s).astype(jnp.bfloat16)
                twisted[place, below, lanes] = (upper * s + lower * c).astype(jnp.bfloat16)

    def finish(slot, place):
        mass = indices_ref[slot] % 64
        norm = jnp.sum(jnp.where(lane_id == mass, norm_row, 0.0), axis=1, keepdims=True)
        scale = lax.rsqrt(norm) * jnp.where(slot < count, 1.0, 0.0)
        for side in range(2):
            result = jnp.dot(
                last_ref[side],
                twisted[place, :, 256 * side : 256 * side + 256],
                preferred_element_type=jnp.float32,
            )
            scaled = result[: 2 * COLS] * scale
            for i in range(2):
                series[2 * side + i, pl.ds(slot, 2 * COLS, stride=TPL_DEV), :] = scaled[
                    :, 128 * i : 128 * i + 128
                ]

    @pl.loop(0, batches)
    def _(batch):
        for place in range(BATCH):
            multiply(batch, place)

        for place in range(STORED):
            later = (batch + 2) * STORED + place

            @pl.when(later < steps)
            def _():
                fetch(later).start()

        for parity in range(2):
            middle[parity] = jnp.dot(
                products[parity], first_ref[parity], preferred_element_type=jnp.float32
            )
        for place in range(BATCH):
            twist(place)
        for place in range(BATCH):
            finish(batch * BATCH + place, place)

    def write(out_ref, half, shifted):
        def tile_of(part, index):
            column, tile = divmod(index, 4)
            start = (part * COLS + 4 * half + column) * TPL_DEV
            return series[tile, pl.ds(pl.multiple_of(start, TPL_DEV), TPL_DEV), :]

        lower = lax.broadcasted_iota(jnp.int32, (TPL_DEV, 128), 1) < 64
        for part in range(2):
            before = None
            for i in range(SPAN // 128):
                tile = tile_of(part, 4 + i)
                if shifted:
                    if before is None:
                        before = pltpu.roll(tile_of(part, 3), 64, axis=1)
                    turned = pltpu.roll(tile, 64, axis=1)
                    tile, before = jnp.where(lower, before, turned), turned
                out_ref[part, :, 128 * i : 128 * i + 128] = tile.astype(jnp.bfloat16)

    for det in range(2):

        @pl.when(half_ref[0] == det)
        def _():
            write(own_ref, det, det == 1)
            write(send_ref, 1 - det, det == 1)


def coherent_kernel(
    half_ref,
    delay_ref,
    near_gain_ref,
    far_gain_ref,
    own_ref,
    got_ref,
    out_ref,
    near,
    pairs,
    tiles,
    sems,
):
    def unpack(near_ref, far_ref):
        for tile in range(TILES):
            for part in range(2):
                rows = slice(32 * tile + 16 * part, 32 * tile + 16 * part + 16)
                near[rows, :] = near_ref[part, :, 128 * tile : 128 * tile + 128].astype(jnp.float32)
                pairs[rows, :] = far_ref[part, :, 128 * tile : 128 * tile + 256]

    @pl.when(half_ref[0] == 0)
    def _():
        unpack(own_ref, got_ref.at[1])

    @pl.when(half_ref[0] == 1)
    def _():
        unpack(got_ref.at[0], own_ref)

    row_id = lax.broadcasted_iota(jnp.int32, (256, 256), 0)
    col_id = lax.broadcasted_iota(jnp.int32, (256, 256), 1)

    def copy_out(tile):
        lanes = slice(128 * tile, 128 * tile + 128)
        return pltpu.make_async_copy(tiles.at[tile], out_ref.at[:, lanes], sems.at[tile])

    for group in range(0, TILES, GROUP):
        for sky in range(0, SKY, 2):
            shift = jnp.where(col_id < 128, delay_ref[sky] + 64, delay_ref[sky + 1] - 64)
            pick = jnp.where(row_id == col_id + shift, 1.0, 0.0).astype(jnp.bfloat16)
            delayed = jnp.dot(
                pairs[32 * group : 32 * (group + GROUP), :],
                pick,
                preferred_element_type=jnp.float32,
            )
            for side in range(2):
                gain_near, gain_far = near_gain_ref[sky + side], far_gain_ref[sky + side]
                power = gain_near * gain_near + gain_far * gain_far
                inverse = lax.rsqrt(jnp.full((1, 128), power, jnp.float32))
                near_row = jnp.broadcast_to(gain_near * inverse, (TPL_DEV, 128))
                far_row = jnp.broadcast_to(gain_far * inverse, (TPL_DEV, 128))
                lanes = slice(128 * side, 128 * side + 128)
                for i in range(GROUP):
                    tile = group + i
                    re, im = (
                        near_row * near[32 * tile + at : 32 * tile + at + 16, :]
                        + far_row * delayed[32 * i + at : 32 * i + at + 16, lanes]
                        for at in (0, 16)
                    )
                    place = pl.ds(sky + side, TPL_DEV, stride=SKY)
                    tiles[tile, place, :] = re * re + im * im
        for i in range(GROUP):
            copy_out(group + i).start()

    for tile in range(TILES):
        copy_out(tile).wait()


ANY = pl.BlockSpec(memory_space=pl.ANY)
VMEM = pl.BlockSpec(memory_space=pltpu.VMEM)
SMEM = pl.BlockSpec(memory_space=pltpu.SMEM)


def on_device(strain, asd_inv, indices, counts, sky_delay, gain_near, gain_far):
    powers, first_tables, twist, last, scalars = constant_tables()
    z_groups, xy_groups = group_lists()
    bank = lax.axis_index("bank").astype(jnp.int32)[None]
    half = lax.axis_index("det").astype(jnp.int32)[None]
    payload = pl.pallas_call(
        prepare_kernel,
        out_shape=jax.ShapeDtypeStruct((N_Z, 1, PAYLOAD), jnp.float32),
        in_specs=[SMEM, VMEM, VMEM],
        out_specs=VMEM,
        compiler_params=pltpu.CompilerParams(vmem_limit_bytes=BIG),
    )(bank, strain[0], asd_inv)
    line = lax.all_to_all(payload, "bank", 0, 0, axis_index_groups=z_groups)
    spread = pl.pallas_call(
        spread_kernel,
        out_shape=jax.ShapeDtypeStruct((N_XY, N_Z, PAYLOAD), jnp.bfloat16),
        in_specs=[VMEM],
        out_specs=VMEM,
    )(line)
    plane = lax.all_to_all(spread, "bank", 0, 0, axis_index_groups=xy_groups)
    waves = pl.pallas_call(
        wave_kernel,
        out_shape=jax.ShapeDtypeStruct((WAVE_ROOM, 2, DFT_COLS, 256), jnp.bfloat16),
        in_specs=[SMEM] * 3 + [ANY],
        out_specs=ANY,
        scratch_shapes=[
            pltpu.VMEM((5, DFT_COLS, 256), jnp.float32),
            pltpu.VMEM((STAGES, 2, DFT_COLS, 256), jnp.bfloat16),
            pltpu.SemaphoreType.DMA((STAGES + 4,)),
        ],
        cost_estimate=pl.CostEstimate(
            flops=40 * 2**20, bytes_accessed=10 * 2**20, transcendentals=2**20
        ),
        compiler_params=pltpu.CompilerParams(vmem_limit_bytes=BIG),
    )(indices, counts, scalars, powers)
    window = jax.ShapeDtypeStruct((2, TPL_DEV, SPAN), jnp.bfloat16)
    own, send = pl.pallas_call(
        filter_kernel,
        out_shape=(window, window),
        in_specs=[SMEM] * 4 + [VMEM] * 5 + [ANY],
        out_specs=(VMEM, VMEM),
        scratch_shapes=[
            pltpu.VMEM((2, DFT_COLS, 256), jnp.float32),
            pltpu.VMEM((2, BATCH * DFT_COLS, 256), jnp.bfloat16),
            pltpu.VMEM((2, BATCH * DFT_COLS, 512), jnp.float32),
            pltpu.VMEM((BATCH, 512, 512), jnp.bfloat16),
            pltpu.VMEM((4, 2 * COLS * TPL_DEV, 128), jnp.float32),
            pltpu.VMEM((2 * STORED, 2, DFT_COLS, 256), jnp.bfloat16),
            pltpu.SemaphoreType.DMA((2 * STORED,)),
        ],
        compiler_params=pltpu.CompilerParams(vmem_limit_bytes=FILTER_VMEM),
    )(indices, counts, half, scalars, plane, first_tables, twist, last, powers, waves)
    got = lax.all_gather(send, "det", axis=0)
    out = pl.pallas_call(
        coherent_kernel,
        out_shape=jax.ShapeDtypeStruct((TPL_DEV * SKY, HALF), jnp.float32),
        in_specs=[SMEM] * 4 + [VMEM] * 2,
        out_specs=pl.BlockSpec(memory_space=pl.ANY),
        scratch_shapes=[
            pltpu.VMEM((2 * TPL_DEV * TILES, 128), jnp.float32),
            pltpu.VMEM((2 * TPL_DEV * TILES, 256), jnp.bfloat16),
            pltpu.VMEM((TILES, TPL_DEV * SKY, 128), jnp.float32),
            pltpu.SemaphoreType.DMA((TILES,)),
        ],
        compiler_params=pltpu.CompilerParams(vmem_limit_bytes=16 * 1024 * 1024),
    )(half, sky_delay, gain_near, gain_far, own, got)
    return out.reshape(TPL_DEV, SKY, HALF)


def solution(mesh):
    return jax.shard_map(
        on_device,
        mesh=mesh,
        in_specs=(P("det", None, "bank"), P("det", "bank"), P("bank"), P("bank"), P(), P(), P()),
        out_specs=P("bank", None, "det"),
        check_vma=False,
    )
```

```python
import functools
import math

import jax
import jax.numpy as jnp
import numpy as np
from jax import lax
from jax.experimental import pallas as pl
from jax.experimental.pallas import tpu as pltpu
from jax.sharding import PartitionSpec as P

DFT_ROWS = 512
DFT_COLS = 256
SAMPLES = 131072
LOW_BIN = 1920
WIN_BLOCKS = 8
WINDOW = 4096
HALF = WINDOW // 2
TPL_DEV = 16
SKY = 16
MASSES = 64
N_Z = 16
N_XY = 16
COLS = WIN_BLOCKS + 2
SPAN = HALF + 128
PAYLOAD = 640
STRIP = 16
BATCH = 4
EARLY = 5
TILES = HALF // 128
GROUP = 8
STAGES = 4
BIG = 60 * 1024 * 1024
FILTER_VMEM = 46 * 1024 * 1024
WAVE_ROOM = 80

MSUN_SEC = 4.925491e-06
SAMPLE_RATE = 2048.0

Z_ORDER = [9, 11, 13, 15, 1, 3, 5, 7, 8, 10, 12, 14, 0, 2, 4, 6]
XY_ORDER = [(k + 5) % N_XY for k in range(N_XY)]


def group_lists():
    z_groups = [[q * N_Z + z for z in Z_ORDER] for q in range(N_XY)]
    xy_groups = [[q * N_Z + z for q in XY_ORDER] for z in range(N_Z)]
    return z_groups, xy_groups


def constant_tables():
    rows = np.array([[q * N_Z + z for z in Z_ORDER] for q in XY_ORDER])
    odd, even = rows[:, :8].reshape(-1), rows[:, 8:].reshape(-1)
    k1 = np.concatenate([odd, even])
    k2 = np.arange(DFT_COLS)
    bins = 256 * k1[None, :] + k2[:, None]
    freq = np.maximum(bins * (SAMPLE_RATE / SAMPLES), 1.0)
    powers = np.stack(
        [
            freq ** (-5.0 / 3.0),
            freq**-1.0,
            freq ** (-2.0 / 3.0),
            np.where(bins >= LOW_BIN, freq ** (-7.0 / 6.0), 0.0),
            freq**4,
        ]
    ).astype(np.float32)

    t1 = np.arange(256)

    def first(rows_k):
        angle = 2.0 * np.pi / 512 * (rows_k[:, None] * t1[None, :] % 512)
        c, s = np.cos(angle), np.sin(angle)
        return np.concatenate([np.concatenate([c, s], 1), np.concatenate([-s, c], 1)], 0)

    first_tables = np.stack([first(odd), first(even)])
    angle = 2.0 * np.pi / SAMPLES * (k2[:, None] * t1[None, :] % SAMPLES)
    twist = np.stack([np.cos(angle), np.sin(angle)]).astype(np.float32)
    t2 = DFT_COLS // 2 - WIN_BLOCKS // 2 - 1 + np.arange(COLS)
    last = np.zeros((2, 32, 512))
    for side in range(2):
        steps = k2[None, :] * (t2[:, None] * DFT_ROWS + 256 * side)
        angle = 2.0 * np.pi / SAMPLES * (steps % SAMPLES)
        c, s = np.cos(angle), np.sin(angle)
        last[side, :COLS] = np.concatenate([c, -s], 1)
        last[side, COLS : 2 * COLS] = np.concatenate([s, c], 1)

    seconds = 6.0 * 1.03 ** np.arange(MASSES) * MSUN_SEC
    ratio = 0.16 + 0.09 * np.arange(64) / 63.0
    x = np.pi * seconds
    turn = 1.0 / (2.0 * np.pi)
    scalars = np.stack(
        [
            turn * x ** (-5.0 / 3.0),
            turn * x**-1.0,
            turn * x ** (-2.0 / 3.0),
            -((6.0**1.5 * x) ** 4) / math.log(2.0),
            3.0 / (128.0 * ratio),
            3715.0 / 756.0 + 55.0 * ratio / 9.0,
            (113.0 - 76.0 * ratio) / 12.0,
            np.zeros(64),
        ]
    ).astype(np.float32)
    return (
        powers,
        first_tables.astype(jnp.bfloat16),
        twist,
        last.astype(jnp.bfloat16),
        scalars,
    )


def even_fit(function, terms):
    nodes = 0.5 * np.cos(np.pi * (np.arange(400) + 0.5) / 400)
    design = (nodes[:, None] ** 2) ** np.arange(terms)[None, :]
    fitted = np.linalg.lstsq(design, function(nodes), rcond=None)[0]
    return [float(np.float32(v)) for v in fitted]


ROOT2 = math.sqrt(2.0)
SIN_FIT = even_fit(lambda r: ROOT2 * np.pi * np.sinc(r), 5)
ROUND_SHIFT = 12582912.0


def horner(coefs, square):
    total = coefs[-1] * square + coefs[-2]
    for c in coefs[-3::-1]:
        total = total * square + c
    return total


def payload_row(bank, strain, asd):
    weight = asd * asd
    over = strain * weight
    bin_id = bank * 256 + lax.broadcasted_iota(jnp.int32, (1, 256), 1)
    clipped = jnp.maximum(bin_id.astype(jnp.float32) * (SAMPLE_RATE / SAMPLES), 1.0)
    square = clipped * clipped
    falling = jnp.exp((-7.0 / 3.0) * jnp.log(clipped))
    weighted = jnp.where(bin_id >= LOW_BIN, falling, 0.0) * weight
    mass_id = lax.broadcasted_iota(jnp.int32, (MASSES, 1), 0).astype(jnp.float32)
    start = math.log(2.0) + 4.0 * math.log(6.0**1.5 * math.pi * 6.0 * MSUN_SEC)
    steep = jnp.exp(4.0 * math.log(1.03) * mass_id + start)
    column = jnp.sum(jnp.exp(-steep * (square * square)) * weighted, axis=1, keepdims=True)
    row_id = lax.broadcasted_iota(jnp.int32, (MASSES, MASSES), 0)
    col_id = lax.broadcasted_iota(jnp.int32, (MASSES, MASSES), 1)
    norms = jnp.sum(jnp.where(row_id == col_id, column, 0.0), axis=0, keepdims=True)
    coarse = norms.astype(jnp.bfloat16).astype(jnp.float32)
    return jnp.concatenate([over[0:1], over[1:2], coarse, norms - coarse], axis=1)


def slot_scalars(slot, indices_ref, scalars_ref):
    entry = indices_ref[slot]
    mass, eta = entry % 64, entry // 64 % 64
    spin = -0.6 + 0.4 * (entry // 4096).astype(jnp.float32)
    lead = scalars_ref[4, eta]
    c53 = lead * scalars_ref[0, mass]
    c1 = lead * scalars_ref[5, eta] * scalars_ref[1, mass]
    c23 = lead * (4.0 * spin * scalars_ref[6, eta] - 16.0 * math.pi) * scalars_ref[2, mass]
    return c53, c1, c23, scalars_ref[3, mass]


def wave(coefs, powers, here):
    c53, c1, c23, steep = coefs
    turns = (
        c53 * powers[0, here, :] + c1 * powers[1, here, :] + (c23 * powers[2, here, :] - 0.125)
    )
    rest = turns - ((turns + ROUND_SHIFT) - ROUND_SHIFT)
    square = rest * rest
    half_sin = horner(SIN_FIT, square) * rest
    cosine = 1.0 - half_sin * half_sin
    above = jnp.maximum(1.0 + cosine, 1e-12)
    half_cos = above * lax.rsqrt(above)
    envelope = powers[3, here, :] * jnp.exp2(steep * powers[4, here, :])
    return envelope * cosine, envelope * (half_sin * half_cos)


def early_slots(bank, count):
    z = bank % N_Z
    early = jnp.where(z < 4, EARLY, jnp.where(z < 7, EARLY // 2, 0))
    return jnp.minimum(early, rounded_up(count))


def wave_kernel(
    bank_ref,
    indices_ref,
    counts_ref,
    scalars_ref,
    powers_hbm,
    early_ref,
    waves_ref,
    powers,
    staged,
    sems,
):
    first, last = early_slots(bank_ref[0], counts_ref[0]), rounded_up(counts_ref[0])
    write_waves(first, last, indices_ref, scalars_ref, powers_hbm, waves_ref, powers, staged, sems)


def write_waves(first, last, indices_ref, scalars_ref, powers_hbm, waves_ref, powers, staged, sems):
    def store(slot):
        place = slot % STAGES
        return pltpu.make_async_copy(staged.at[place], waves_ref.at[slot], sems.at[place])

    def load(strip):
        rows = pl.ds(strip * 64, 64)
        return pltpu.make_async_copy(
            powers_hbm.at[:, rows], powers.at[:, rows], sems.at[STAGES + strip]
        )

    @pl.when(last > first)
    def _():
        for strip in range(4):
            load(strip).start()

    @pl.loop(first, last)
    def _(slot):
        coefs = slot_scalars(slot, indices_ref, scalars_ref)

        @pl.when(slot >= first + STAGES)
        def _():
            store(slot - STAGES).wait()

        @pl.loop(0, DFT_COLS // 64)
        def _(strip):
            @pl.when(slot == first)
            def _():
                load(strip).wait()

            for piece in range(4):
                here = pl.ds(pl.multiple_of(strip * 64 + piece * 16, 16), 16)
                cosine, sine = wave(coefs, powers, here)
                staged[slot % STAGES, 0, here, :] = cosine.astype(jnp.bfloat16)
                staged[slot % STAGES, 1, here, :] = sine.astype(jnp.bfloat16)

        store(slot).start()

    for back in range(STAGES, 0, -1):

        @pl.when(last - first >= back)
        def _():
            store(last - back).wait()


def rounded_up(count):
    return (count + BATCH - 1) // BATCH * BATCH


def prepare_kernel(
    bank_ref,
    indices_ref,
    counts_ref,
    scalars_ref,
    strain_ref,
    asd_ref,
    powers_hbm,
    out_ref,
    waves_ref,
    powers,
    staged,
    sems,
):
    row = payload_row(bank_ref[0], strain_ref[...], asd_ref[...])
    pair = jnp.concatenate([row[:, : PAYLOAD // 2], row[:, PAYLOAD // 2 :]], axis=0)
    out_ref[...] = jnp.broadcast_to(pair.astype(jnp.bfloat16)[None], out_ref.shape)
    last = early_slots(bank_ref[0], counts_ref[0])
    write_waves(0, last, indices_ref, scalars_ref, powers_hbm, waves_ref, powers, staged, sems)


def filter_kernel(
    indices_ref,
    counts_ref,
    half_ref,
    gathered_ref,
    first_ref,
    twist_ref,
    last_ref,
    waves_ref,
    own_ref,
    send_ref,
    spectrum,
    products,
    middle,
    twisted,
    series,
    waves,
    sems,
):
    count = counts_ref[0]
    slots = rounded_up(count)

    def fetch(slot):
        place = slot % (2 * BATCH)
        return pltpu.make_async_copy(waves_ref.at[slot], waves.at[place], sems.at[place])

    def fetch_batch(batch):
        for place in range(BATCH):
            fetch(batch * BATCH + place).start()

    fetch_batch(0)

    for part in range(2):
        block = gathered_ref[:, :, 256 * part : 256 * part + 256].astype(jnp.float32)
        for parity in range(2):
            rows = block[:, 8 * parity : 8 * parity + 8].reshape(128, 256)
            spectrum[part, :, 128 * parity : 128 * parity + 128] = rows.T
    sums = jnp.sum(
        gathered_ref[:, :, 512:640].astype(jnp.float32).reshape(256, 128), axis=0, keepdims=True
    )
    norm_row = sums[:, :MASSES] + sums[:, MASSES:]
    lane_id = lax.broadcasted_iota(jnp.int32, (1, MASSES), 1)
    series[...] = jnp.zeros_like(series)

    def multiply(slot, place):
        buffer = slot % (2 * BATCH)
        fetch(slot).wait()
        for i in range(0, DFT_COLS, STRIP):
            here, there = slice(i, i + STRIP), slice(256 * place + i, 256 * place + i + STRIP)
            cosine = waves[buffer, 0, here, :].astype(jnp.float32)
            sine = waves[buffer, 1, here, :].astype(jnp.float32)
            re, im = spectrum[0, here, :], spectrum[1, here, :]
            real_part = (re * cosine - im * sine).astype(jnp.bfloat16)
            imag_part = (re * sine + im * cosine).astype(jnp.bfloat16)
            for parity in range(2):
                lanes = slice(128 * parity, 128 * parity + 128)
                products[parity, there, 0:128] = real_part[:, lanes]
                products[parity, there, 128:256] = imag_part[:, lanes]

    def twist(place):
        for i in range(0, DFT_COLS, STRIP):
            here, below = slice(i, i + STRIP), slice(256 + i, 256 + i + STRIP)
            there = slice(256 * place + i, 256 * place + i + STRIP)
            odd_re, odd_im = middle[0, there, 0:256], middle[0, there, 256:512]
            even_re, even_im = middle[1, there, 0:256], middle[1, there, 256:512]
            c, s = twist_ref[0, here, :], twist_ref[1, here, :]
            for side in range(2):
                lanes = slice(256 * side, 256 * side + 256)
                upper = even_re - odd_re if side else even_re + odd_re
                lower = even_im - odd_im if side else even_im + odd_im
                twisted[place, here, lanes] = (upper * c - lower * s).astype(jnp.bfloat16)
                twisted[place, below, lanes] = (upper * s + lower * c).astype(jnp.bfloat16)

    def finish(slot, place):
        mass = indices_ref[slot] % 64
        norm = jnp.sum(jnp.where(lane_id == mass, norm_row, 0.0), axis=1, keepdims=True)
        scale = lax.rsqrt(norm) * jnp.where(slot < count, 1.0, 0.0)
        for side in range(2):
            result = jnp.dot(
                last_ref[side],
                twisted[place, :, 256 * side : 256 * side + 256],
                preferred_element_type=jnp.float32,
            )
            scaled = result[: 2 * COLS] * scale
            for i in range(2):
                series[2 * side + i, pl.ds(slot, 2 * COLS, stride=TPL_DEV), :] = scaled[
                    :, 128 * i : 128 * i + 128
                ]

    @pl.loop(0, slots // BATCH)
    def _(batch):
        @pl.when((batch + 1) * BATCH < slots)
        def _():
            fetch_batch(batch + 1)

        for place in range(BATCH):
            multiply(batch * BATCH + place, place)
        for parity in range(2):
            middle[parity] = jnp.dot(
                products[parity], first_ref[parity], preferred_element_type=jnp.float32
            )
        for place in range(BATCH):
            twist(place)
        for place in range(BATCH):
            finish(batch * BATCH + place, place)

    def write(out_ref, half, shifted):
        def tile_of(part, index):
            column, tile = divmod(index, 4)
            start = (part * COLS + 4 * half + column) * TPL_DEV
            return series[tile, pl.ds(pl.multiple_of(start, TPL_DEV), TPL_DEV), :]

        lower = lax.broadcasted_iota(jnp.int32, (TPL_DEV, 128), 1) < 64
        for part in range(2):
            before = None
            for i in range(SPAN // 128):
                tile = tile_of(part, 4 + i)
                if shifted:
                    if before is None:
                        before = pltpu.roll(tile_of(part, 3), 64, axis=1)
                    turned = pltpu.roll(tile, 64, axis=1)
                    tile, before = jnp.where(lower, before, turned), turned
                out_ref[part, :, 128 * i : 128 * i + 128] = tile.astype(jnp.bfloat16)

    for det in range(2):

        @pl.when(half_ref[0] == det)
        def _():
            write(own_ref, det, det == 1)
            write(send_ref, 1 - det, det == 1)


def coherent_kernel(
    half_ref,
    delay_ref,
    near_gain_ref,
    far_gain_ref,
    own_ref,
    got_ref,
    out_ref,
    near,
    pairs,
    tiles,
    sems,
):
    def unpack(near_ref, far_ref):
        for tile in range(TILES):
            for part in range(2):
                rows = slice(32 * tile + 16 * part, 32 * tile + 16 * part + 16)
                near[rows, :] = near_ref[part, :, 128 * tile : 128 * tile + 128].astype(jnp.float32)
                pairs[rows, :] = far_ref[part, :, 128 * tile : 128 * tile + 256]

    @pl.when(half_ref[0] == 0)
    def _():
        unpack(own_ref, got_ref.at[1])

    @pl.when(half_ref[0] == 1)
    def _():
        unpack(got_ref.at[0], own_ref)

    row_id = lax.broadcasted_iota(jnp.int32, (256, 256), 0)
    col_id = lax.broadcasted_iota(jnp.int32, (256, 256), 1)

    def copy_out(tile):
        lanes = slice(128 * tile, 128 * tile + 128)
        return pltpu.make_async_copy(tiles.at[tile], out_ref.at[:, lanes], sems.at[tile])

    for group in range(0, TILES, GROUP):
        for sky in range(0, SKY, 2):
            shift = jnp.where(col_id < 128, delay_ref[sky] + 64, delay_ref[sky + 1] - 64)
            pick = jnp.where(row_id == col_id + shift, 1.0, 0.0).astype(jnp.bfloat16)
            delayed = jnp.dot(
                pairs[32 * group : 32 * (group + GROUP), :],
                pick,
                preferred_element_type=jnp.float32,
            )
            for side in range(2):
                gain_near, gain_far = near_gain_ref[sky + side], far_gain_ref[sky + side]
                power = gain_near * gain_near + gain_far * gain_far
                inverse = lax.rsqrt(jnp.full((1, 128), power, jnp.float32))
                near_row = jnp.broadcast_to(gain_near * inverse, (TPL_DEV, 128))
                far_row = jnp.broadcast_to(gain_far * inverse, (TPL_DEV, 128))
                lanes = slice(128 * side, 128 * side + 128)
                for i in range(GROUP):
                    tile = group + i
                    re, im = (
                        near_row * near[32 * tile + at : 32 * tile + at + 16, :]
                        + far_row * delayed[32 * i + at : 32 * i + at + 16, lanes]
                        for at in (0, 16)
                    )
                    place = pl.ds(sky + side, TPL_DEV, stride=SKY)
                    tiles[tile, place, :] = re * re + im * im
        for i in range(GROUP):
            copy_out(group + i).start()

    for tile in range(TILES):
        copy_out(tile).wait()


ANY = pl.BlockSpec(memory_space=pl.ANY)
VMEM = pl.BlockSpec(memory_space=pltpu.VMEM)
SMEM = pl.BlockSpec(memory_space=pltpu.SMEM)


def on_device(strain, asd_inv, indices, counts, sky_delay, gain_near, gain_far):
    powers, first_tables, twist, last, scalars = constant_tables()
    z_groups, xy_groups = group_lists()
    bank = lax.axis_index("bank").astype(jnp.int32)[None]
    half = lax.axis_index("det").astype(jnp.int32)[None]
    room = jax.ShapeDtypeStruct((WAVE_ROOM, 2, DFT_COLS, 256), jnp.bfloat16)
    wave_scratch = [
        pltpu.VMEM((5, DFT_COLS, 256), jnp.float32),
        pltpu.VMEM((STAGES, 2, DFT_COLS, 256), jnp.bfloat16),
        pltpu.SemaphoreType.DMA((STAGES + 4,)),
    ]
    payload, early = pl.pallas_call(
        prepare_kernel,
        out_shape=(jax.ShapeDtypeStruct((N_Z, 2, PAYLOAD // 2), jnp.bfloat16), room),
        in_specs=[SMEM] * 4 + [VMEM] * 2 + [ANY],
        out_specs=(VMEM, ANY),
        scratch_shapes=wave_scratch,
        compiler_params=pltpu.CompilerParams(vmem_limit_bytes=BIG),
    )(bank, indices, counts, scalars, strain[0], asd_inv, powers)
    line = lax.all_to_all(payload, "bank", 0, 0, axis_index_groups=z_groups)
    spread = jnp.broadcast_to(line.reshape(1, N_Z, PAYLOAD), (N_XY, N_Z, PAYLOAD))
    plane = lax.all_to_all(spread, "bank", 0, 0, axis_index_groups=xy_groups)
    waves = pl.pallas_call(
        wave_kernel,
        out_shape=room,
        in_specs=[SMEM] * 4 + [ANY] * 2,
        out_specs=ANY,
        scratch_shapes=wave_scratch,
        input_output_aliases={5: 0},
        cost_estimate=pl.CostEstimate(
            flops=40 * 2**20, bytes_accessed=10 * 2**20, transcendentals=2**20
        ),
        compiler_params=pltpu.CompilerParams(vmem_limit_bytes=BIG),
    )(bank, indices, counts, scalars, powers, early)
    window = jax.ShapeDtypeStruct((2, TPL_DEV, SPAN), jnp.bfloat16)
    own, send = pl.pallas_call(
        filter_kernel,
        out_shape=(window, window),
        in_specs=[SMEM] * 3 + [VMEM] * 4 + [ANY],
        out_specs=(VMEM, VMEM),
        scratch_shapes=[
            pltpu.VMEM((2, DFT_COLS, 256), jnp.float32),
            pltpu.VMEM((2, BATCH * DFT_COLS, 256), jnp.bfloat16),
            pltpu.VMEM((2, BATCH * DFT_COLS, 512), jnp.float32),
            pltpu.VMEM((BATCH, 512, 512), jnp.bfloat16),
            pltpu.VMEM((4, 2 * COLS * TPL_DEV, 128), jnp.float32),
            pltpu.VMEM((2 * BATCH, 2, DFT_COLS, 256), jnp.bfloat16),
            pltpu.SemaphoreType.DMA((2 * BATCH,)),
        ],
        compiler_params=pltpu.CompilerParams(vmem_limit_bytes=FILTER_VMEM),
    )(indices, counts, half, plane, first_tables, twist, last, waves)
    got = lax.all_gather(send, "det", axis=0)
    out = pl.pallas_call(
        coherent_kernel,
        out_shape=jax.ShapeDtypeStruct((TPL_DEV * SKY, HALF), jnp.float32),
        in_specs=[SMEM] * 4 + [VMEM] * 2,
        out_specs=pl.BlockSpec(memory_space=pl.ANY),
        scratch_shapes=[
            pltpu.VMEM((2 * TPL_DEV * TILES, 128), jnp.float32),
            pltpu.VMEM((2 * TPL_DEV * TILES, 256), jnp.bfloat16),
            pltpu.VMEM((TILES, TPL_DEV * SKY, 128), jnp.float32),
            pltpu.SemaphoreType.DMA((TILES,)),
        ],
        compiler_params=pltpu.CompilerParams(vmem_limit_bytes=16 * 1024 * 1024),
    )(half, sky_delay, gain_near, gain_far, own, got)
    return out.reshape(TPL_DEV, SKY, HALF)


def solution(mesh):
    return jax.shard_map(
        on_device,
        mesh=mesh,
        in_specs=(P("det", None, "bank"), P("det", "bank"), P("bank"), P("bank"), P(), P(), P()),
        out_specs=P("bank", None, "det"),
        check_vma=False,
    )
```

```python
import functools
import math

import jax
import jax.numpy as jnp
import numpy as np
from jax import lax
from jax.experimental import pallas as pl
from jax.experimental.pallas import tpu as pltpu
from jax.sharding import PartitionSpec as P

DFT_ROWS = 512
DFT_COLS = 256
SAMPLES = 131072
LOW_BIN = 1920
WIN_BLOCKS = 8
WINDOW = 4096
HALF = WINDOW // 2
TPL_DEV = 16
SKY = 16
MASSES = 64
N_Z = 16
N_XY = 16
COLS = WIN_BLOCKS + 2
SPAN = HALF + 128
PAYLOAD = 640
STRIP = 16
BATCH = 8
LAST_ROWS = 24
EARLY = 5
TILES = HALF // 128
GROUP = 8
STAGES = 4
BIG = 60 * 1024 * 1024
FILTER_VMEM = 46 * 1024 * 1024
WAVE_ROOM = 80

MSUN_SEC = 4.925491e-06
SAMPLE_RATE = 2048.0

Z_ORDER = [9, 11, 13, 15, 1, 3, 5, 7, 8, 10, 12, 14, 0, 2, 4, 6]
XY_ORDER = [(k + 5) % N_XY for k in range(N_XY)]


def group_lists():
    z_groups = [[q * N_Z + z for z in Z_ORDER] for q in range(N_XY)]
    xy_groups = [[q * N_Z + z for q in XY_ORDER] for z in range(N_Z)]
    return z_groups, xy_groups


def constant_tables():
    rows = np.array([[q * N_Z + z for z in Z_ORDER] for q in XY_ORDER])
    odd, even = rows[:, :8].reshape(-1), rows[:, 8:].reshape(-1)
    k1 = np.concatenate([odd, even])
    k2 = np.arange(DFT_COLS)
    bins = 256 * k1[None, :] + k2[:, None]
    freq = np.maximum(bins * (SAMPLE_RATE / SAMPLES), 1.0)
    powers = np.stack(
        [
            freq ** (-5.0 / 3.0),
            freq**-1.0,
            freq ** (-2.0 / 3.0),
            np.where(bins >= LOW_BIN, freq ** (-7.0 / 6.0), 0.0),
            freq**4,
        ]
    ).astype(np.float32)

    t1 = np.arange(256)

    def first(rows_k):
        angle = 2.0 * np.pi / 512 * (rows_k[:, None] * t1[None, :] % 512)
        c, s = np.cos(angle), np.sin(angle)
        return np.concatenate([np.concatenate([c, s], 1), np.concatenate([-s, c], 1)], 0)

    first_tables = np.stack([first(odd), first(even)])
    angle = 2.0 * np.pi / SAMPLES * (k2[:, None] * t1[None, :] % SAMPLES)
    twist = np.stack([np.cos(angle), np.sin(angle)]).astype(np.float32)
    t2 = DFT_COLS // 2 - WIN_BLOCKS // 2 - 1 + np.arange(COLS)
    last = np.zeros((2 * LAST_ROWS, 1024))
    for side in range(2):
        steps = k2[None, :] * (t2[:, None] * DFT_ROWS + 256 * side)
        angle = 2.0 * np.pi / SAMPLES * (steps % SAMPLES)
        c, s = np.cos(angle), np.sin(angle)
        rows = np.concatenate([np.concatenate([c, -s], 1), np.concatenate([s, c], 1)], 0)
        at = LAST_ROWS * side
        last[at : at + 2 * COLS] = np.concatenate([-rows if side else rows, rows], 1)

    seconds = 6.0 * 1.03 ** np.arange(MASSES) * MSUN_SEC
    ratio = 0.16 + 0.09 * np.arange(64) / 63.0
    x = np.pi * seconds
    turn = 1.0 / (2.0 * np.pi)
    scalars = np.stack(
        [
            turn * x ** (-5.0 / 3.0),
            turn * x**-1.0,
            turn * x ** (-2.0 / 3.0),
            -((6.0**1.5 * x) ** 4) / math.log(2.0),
            3.0 / (128.0 * ratio),
            3715.0 / 756.0 + 55.0 * ratio / 9.0,
            (113.0 - 76.0 * ratio) / 12.0,
            np.zeros(64),
        ]
    ).astype(np.float32)
    return (
        powers,
        first_tables.astype(jnp.bfloat16),
        twist,
        last.astype(jnp.bfloat16),
        scalars,
    )


def even_fit(function, terms):
    nodes = 0.5 * np.cos(np.pi * (np.arange(400) + 0.5) / 400)
    design = (nodes[:, None] ** 2) ** np.arange(terms)[None, :]
    fitted = np.linalg.lstsq(design, function(nodes), rcond=None)[0]
    return [float(np.float32(v)) for v in fitted]


ROOT2 = math.sqrt(2.0)
SIN_FIT = even_fit(lambda r: ROOT2 * np.pi * np.sinc(r), 5)
ROUND_SHIFT = 12582912.0


def horner(coefs, square):
    total = coefs[-1] * square + coefs[-2]
    for c in coefs[-3::-1]:
        total = total * square + c
    return total


def payload_row(bank, strain, asd):
    weight = asd * asd
    over = strain * weight
    bin_id = bank * 256 + lax.broadcasted_iota(jnp.int32, (1, 256), 1)
    clipped = jnp.maximum(bin_id.astype(jnp.float32) * (SAMPLE_RATE / SAMPLES), 1.0)
    square = clipped * clipped
    falling = jnp.exp((-7.0 / 3.0) * jnp.log(clipped))
    weighted = jnp.where(bin_id >= LOW_BIN, falling, 0.0) * weight
    mass_id = lax.broadcasted_iota(jnp.int32, (MASSES, 1), 0).astype(jnp.float32)
    start = math.log(2.0) + 4.0 * math.log(6.0**1.5 * math.pi * 6.0 * MSUN_SEC)
    steep = jnp.exp(4.0 * math.log(1.03) * mass_id + start)
    column = jnp.sum(jnp.exp(-steep * (square * square)) * weighted, axis=1, keepdims=True)
    row_id = lax.broadcasted_iota(jnp.int32, (MASSES, MASSES), 0)
    col_id = lax.broadcasted_iota(jnp.int32, (MASSES, MASSES), 1)
    norms = jnp.sum(jnp.where(row_id == col_id, column, 0.0), axis=0, keepdims=True)
    coarse = norms.astype(jnp.bfloat16).astype(jnp.float32)
    return jnp.concatenate([over[0:1], over[1:2], coarse, norms - coarse], axis=1)


def slot_scalars(slot, indices_ref, scalars_ref):
    entry = indices_ref[slot]
    mass, eta = entry % 64, entry // 64 % 64
    spin = -0.6 + 0.4 * (entry // 4096).astype(jnp.float32)
    lead = scalars_ref[4, eta]
    c53 = lead * scalars_ref[0, mass]
    c1 = lead * scalars_ref[5, eta] * scalars_ref[1, mass]
    c23 = lead * (4.0 * spin * scalars_ref[6, eta] - 16.0 * math.pi) * scalars_ref[2, mass]
    return c53, c1, c23, scalars_ref[3, mass]


def wave(coefs, powers, here):
    c53, c1, c23, steep = coefs
    turns = (
        c53 * powers[0, here, :] + c1 * powers[1, here, :] + (c23 * powers[2, here, :] - 0.125)
    )
    rest = turns - ((turns + ROUND_SHIFT) - ROUND_SHIFT)
    square = rest * rest
    half_sin = horner(SIN_FIT, square) * rest
    cosine = 1.0 - half_sin * half_sin
    above = jnp.maximum(1.0 + cosine, 1e-12)
    half_cos = above * lax.rsqrt(above)
    envelope = powers[3, here, :] * jnp.exp2(steep * powers[4, here, :])
    return envelope * cosine, envelope * (half_sin * half_cos)


def early_slots(bank, count):
    z = bank % N_Z
    early = jnp.where(z < 4, EARLY, jnp.where(z < 7, EARLY // 2, 0))
    return jnp.minimum(early, rounded_up(count))


def wave_kernel(
    bank_ref,
    indices_ref,
    counts_ref,
    scalars_ref,
    powers_hbm,
    early_ref,
    waves_ref,
    powers,
    staged,
    sems,
):
    first, last = early_slots(bank_ref[0], counts_ref[0]), rounded_up(counts_ref[0])
    write_waves(first, last, indices_ref, scalars_ref, powers_hbm, waves_ref, powers, staged, sems)


def write_waves(first, last, indices_ref, scalars_ref, powers_hbm, waves_ref, powers, staged, sems):
    def store(slot):
        place = slot % STAGES
        return pltpu.make_async_copy(staged.at[place], waves_ref.at[slot], sems.at[place])

    def load(strip):
        rows = pl.ds(strip * 64, 64)
        return pltpu.make_async_copy(
            powers_hbm.at[:, rows], powers.at[:, rows], sems.at[STAGES + strip]
        )

    @pl.when(last > first)
    def _():
        for strip in range(4):
            load(strip).start()

    @pl.loop(first, last)
    def _(slot):
        coefs = slot_scalars(slot, indices_ref, scalars_ref)

        @pl.when(slot >= first + STAGES)
        def _():
            store(slot - STAGES).wait()

        @pl.loop(0, DFT_COLS // 64)
        def _(strip):
            @pl.when(slot == first)
            def _():
                load(strip).wait()

            for piece in range(4):
                here = pl.ds(pl.multiple_of(strip * 64 + piece * 16, 16), 16)
                cosine, sine = wave(coefs, powers, here)
                staged[slot % STAGES, 0, here, :] = cosine.astype(jnp.bfloat16)
                staged[slot % STAGES, 1, here, :] = sine.astype(jnp.bfloat16)

        store(slot).start()

    for back in range(STAGES, 0, -1):

        @pl.when(last - first >= back)
        def _():
            store(last - back).wait()


def rounded_up(count):
    return (count + BATCH - 1) // BATCH * BATCH


def prepare_kernel(
    bank_ref,
    indices_ref,
    counts_ref,
    scalars_ref,
    strain_ref,
    asd_ref,
    powers_hbm,
    out_ref,
    waves_ref,
    powers,
    staged,
    sems,
):
    row = payload_row(bank_ref[0], strain_ref[...], asd_ref[...])
    pair = jnp.concatenate([row[:, : PAYLOAD // 2], row[:, PAYLOAD // 2 :]], axis=0)
    out_ref[...] = jnp.broadcast_to(pair.astype(jnp.bfloat16)[None], out_ref.shape)
    last = early_slots(bank_ref[0], counts_ref[0])
    write_waves(0, last, indices_ref, scalars_ref, powers_hbm, waves_ref, powers, staged, sems)


def filter_kernel(
    indices_ref,
    counts_ref,
    half_ref,
    gathered_ref,
    first_ref,
    twist_ref,
    last_ref,
    waves_ref,
    own_ref,
    send_ref,
    spectrum,
    products,
    middle,
    twisted,
    series,
    waves,
    sems,
):
    count = counts_ref[0]
    slots = rounded_up(count)

    def fetch(slot):
        place = slot % (2 * BATCH)
        return pltpu.make_async_copy(waves_ref.at[slot], waves.at[place], sems.at[place])

    def fetch_batch(batch):
        for place in range(BATCH):
            fetch(batch * BATCH + place).start()

    fetch_batch(0)

    for part in range(2):
        block = gathered_ref[:, :, 256 * part : 256 * part + 256].astype(jnp.float32)
        for parity in range(2):
            rows = block[:, 8 * parity : 8 * parity + 8].reshape(128, 256)
            spectrum[part, :, 128 * parity : 128 * parity + 128] = rows.T
    sums = jnp.sum(
        gathered_ref[:, :, 512:640].astype(jnp.float32).reshape(256, 128), axis=0, keepdims=True
    )
    norm_row = sums[:, :MASSES] + sums[:, MASSES:]
    lane_id = lax.broadcasted_iota(jnp.int32, (1, MASSES), 1)
    series[...] = jnp.zeros_like(series)

    def multiply(slot, place):
        buffer = slot % (2 * BATCH)
        fetch(slot).wait()
        for i in range(0, DFT_COLS, STRIP):
            here, there = slice(i, i + STRIP), slice(256 * place + i, 256 * place + i + STRIP)
            cosine = waves[buffer, 0, here, :].astype(jnp.float32)
            sine = waves[buffer, 1, here, :].astype(jnp.float32)
            re, im = spectrum[0, here, :], spectrum[1, here, :]
            real_part = (re * cosine - im * sine).astype(jnp.bfloat16)
            imag_part = (re * sine + im * cosine).astype(jnp.bfloat16)
            for parity in range(2):
                lanes = slice(128 * parity, 128 * parity + 128)
                products[parity, there, 0:128] = real_part[:, lanes]
                products[parity, there, 128:256] = imag_part[:, lanes]

    def twist(place, parity):
        for i in range(0, DFT_COLS, STRIP):
            here = slice(i, i + STRIP)
            there = slice(256 * place + i, 256 * place + i + STRIP)
            upper, lower = middle[parity, there, 0:256], middle[parity, there, 256:512]
            c, s = twist_ref[0, here, :], twist_ref[1, here, :]
            at = 512 * parity + i
            twisted[place, at : at + STRIP] = (upper * c - lower * s).astype(jnp.bfloat16)
            twisted[place, at + 256 : at + 256 + STRIP] = (upper * s + lower * c).astype(
                jnp.bfloat16
            )

    def finish(slot, place):
        mass = indices_ref[slot] % 64
        norm = jnp.sum(jnp.where(lane_id == mass, norm_row, 0.0), axis=1, keepdims=True)
        scale = lax.rsqrt(norm) * jnp.where(slot < count, 1.0, 0.0)
        result = scale * jnp.dot(
            last_ref[...], twisted[place], preferred_element_type=jnp.float32
        )
        for side in range(2):
            rows = slice(LAST_ROWS * side, LAST_ROWS * side + 2 * COLS)
            for i in range(2):
                series[2 * side + i, pl.ds(slot, 2 * COLS, stride=TPL_DEV), :] = result[
                    rows, 128 * i : 128 * i + 128
                ]

    @pl.loop(0, slots // BATCH)
    def _(batch):
        @pl.when((batch + 1) * BATCH < slots)
        def _():
            fetch_batch(batch + 1)

        for place in range(BATCH):
            multiply(batch * BATCH + place, place)
        for parity in range(2):
            middle[parity] = jnp.dot(
                products[parity], first_ref[parity], preferred_element_type=jnp.float32
            )
        for parity in range(2):
            for place in range(BATCH):
                twist(place, parity)
        for place in range(BATCH):
            finish(batch * BATCH + place, place)

    def write(out_ref, half, shifted):
        def tile_of(part, index):
            column, tile = divmod(index, 4)
            start = (part * COLS + 4 * half + column) * TPL_DEV
            return series[tile, pl.ds(pl.multiple_of(start, TPL_DEV), TPL_DEV), :]

        lower = lax.broadcasted_iota(jnp.int32, (TPL_DEV, 128), 1) < 64
        for part in range(2):
            before = None
            for i in range(SPAN // 128):
                tile = tile_of(part, 4 + i)
                if shifted:
                    if before is None:
                        before = pltpu.roll(tile_of(part, 3), 64, axis=1)
                    turned = pltpu.roll(tile, 64, axis=1)
                    tile, before = jnp.where(lower, before, turned), turned
                out_ref[part, :, 128 * i : 128 * i + 128] = tile.astype(jnp.bfloat16)

    for det in range(2):

        @pl.when(half_ref[0] == det)
        def _():
            write(own_ref, det, det == 1)
            write(send_ref, 1 - det, det == 1)


def coherent_kernel(
    half_ref,
    delay_ref,
    near_gain_ref,
    far_gain_ref,
    own_ref,
    got_ref,
    out_ref,
    near,
    pairs,
    tiles,
    sems,
):
    def unpack(near_ref, far_ref):
        for tile in range(TILES):
            for part in range(2):
                rows = slice(32 * tile + 16 * part, 32 * tile + 16 * part + 16)
                near[rows, :] = near_ref[part, :, 128 * tile : 128 * tile + 128].astype(jnp.float32)
                pairs[rows, :] = far_ref[part, :, 128 * tile : 128 * tile + 256]

    @pl.when(half_ref[0] == 0)
    def _():
        unpack(own_ref, got_ref.at[1])

    @pl.when(half_ref[0] == 1)
    def _():
        unpack(got_ref.at[0], own_ref)

    row_id = lax.broadcasted_iota(jnp.int32, (256, 256), 0)
    col_id = lax.broadcasted_iota(jnp.int32, (256, 256), 1)

    def copy_out(tile):
        lanes = slice(128 * tile, 128 * tile + 128)
        return pltpu.make_async_copy(tiles.at[tile], out_ref.at[:, lanes], sems.at[tile])

    for group in range(0, TILES, GROUP):
        for sky in range(0, SKY, 2):
            shift = jnp.where(col_id < 128, delay_ref[sky] + 64, delay_ref[sky + 1] - 64)
            pick = jnp.where(row_id == col_id + shift, 1.0, 0.0).astype(jnp.bfloat16)
            delayed = jnp.dot(
                pairs[32 * group : 32 * (group + GROUP), :],
                pick,
                preferred_element_type=jnp.float32,
            )
            for side in range(2):
                gain_near, gain_far = near_gain_ref[sky + side], far_gain_ref[sky + side]
                power = gain_near * gain_near + gain_far * gain_far
                inverse = lax.rsqrt(jnp.full((1, 128), power, jnp.float32))
                near_row = jnp.broadcast_to(gain_near * inverse, (TPL_DEV, 128))
                far_row = jnp.broadcast_to(gain_far * inverse, (TPL_DEV, 128))
                lanes = slice(128 * side, 128 * side + 128)
                for i in range(GROUP):
                    tile = group + i
                    re, im = (
                        near_row * near[32 * tile + at : 32 * tile + at + 16, :]
                        + far_row * delayed[32 * i + at : 32 * i + at + 16, lanes]
                        for at in (0, 16)
                    )
                    place = pl.ds(sky + side, TPL_DEV, stride=SKY)
                    tiles[tile, place, :] = re * re + im * im
        for i in range(GROUP):
            copy_out(group + i).start()

    for tile in range(TILES):
        copy_out(tile).wait()


ANY = pl.BlockSpec(memory_space=pl.ANY)
VMEM = pl.BlockSpec(memory_space=pltpu.VMEM)
SMEM = pl.BlockSpec(memory_space=pltpu.SMEM)


def on_device(strain, asd_inv, indices, counts, sky_delay, gain_near, gain_far):
    powers, first_tables, twist, last, scalars = constant_tables()
    z_groups, xy_groups = group_lists()
    bank = lax.axis_index("bank").astype(jnp.int32)[None]
    half = lax.axis_index("det").astype(jnp.int32)[None]
    room = jax.ShapeDtypeStruct((WAVE_ROOM, 2, DFT_COLS, 256), jnp.bfloat16)
    wave_scratch = [
        pltpu.VMEM((5, DFT_COLS, 256), jnp.float32),
        pltpu.VMEM((STAGES, 2, DFT_COLS, 256), jnp.bfloat16),
        pltpu.SemaphoreType.DMA((STAGES + 4,)),
    ]
    payload, early = pl.pallas_call(
        prepare_kernel,
        out_shape=(jax.ShapeDtypeStruct((N_Z, 2, PAYLOAD // 2), jnp.bfloat16), room),
        in_specs=[SMEM] * 4 + [VMEM] * 2 + [ANY],
        out_specs=(VMEM, ANY),
        scratch_shapes=wave_scratch,
        compiler_params=pltpu.CompilerParams(vmem_limit_bytes=BIG),
    )(bank, indices, counts, scalars, strain[0], asd_inv, powers)
    line = lax.all_to_all(payload, "bank", 0, 0, axis_index_groups=z_groups)
    spread = jnp.broadcast_to(line.reshape(1, N_Z, PAYLOAD), (N_XY, N_Z, PAYLOAD))
    plane = lax.all_to_all(spread, "bank", 0, 0, axis_index_groups=xy_groups)
    waves = pl.pallas_call(
        wave_kernel,
        out_shape=room,
        in_specs=[SMEM] * 4 + [ANY] * 2,
        out_specs=ANY,
        scratch_shapes=wave_scratch,
        input_output_aliases={5: 0},
        cost_estimate=pl.CostEstimate(
            flops=40 * 2**20, bytes_accessed=10 * 2**20, transcendentals=2**20
        ),
        compiler_params=pltpu.CompilerParams(vmem_limit_bytes=BIG),
    )(bank, indices, counts, scalars, powers, early)
    window = jax.ShapeDtypeStruct((2, TPL_DEV, SPAN), jnp.bfloat16)
    own, send = pl.pallas_call(
        filter_kernel,
        out_shape=(window, window),
        in_specs=[SMEM] * 3 + [VMEM] * 4 + [ANY],
        out_specs=(VMEM, VMEM),
        scratch_shapes=[
            pltpu.VMEM((2, DFT_COLS, 256), jnp.float32),
            pltpu.VMEM((2, BATCH * DFT_COLS, 256), jnp.bfloat16),
            pltpu.VMEM((2, BATCH * DFT_COLS, 512), jnp.float32),
            pltpu.VMEM((BATCH, 1024, 256), jnp.bfloat16),
            pltpu.VMEM((4, 2 * COLS * TPL_DEV, 128), jnp.float32),
            pltpu.VMEM((2 * BATCH, 2, DFT_COLS, 256), jnp.bfloat16),
            pltpu.SemaphoreType.DMA((2 * BATCH,)),
        ],
        compiler_params=pltpu.CompilerParams(vmem_limit_bytes=FILTER_VMEM),
    )(indices, counts, half, plane, first_tables, twist, last, waves)
    got = lax.all_gather(send, "det", axis=0)
    out = pl.pallas_call(
        coherent_kernel,
        out_shape=jax.ShapeDtypeStruct((TPL_DEV * SKY, HALF), jnp.float32),
        in_specs=[SMEM] * 4 + [VMEM] * 2,
        out_specs=pl.BlockSpec(memory_space=pl.ANY),
        scratch_shapes=[
            pltpu.VMEM((2 * TPL_DEV * TILES, 128), jnp.float32),
            pltpu.VMEM((2 * TPL_DEV * TILES, 256), jnp.bfloat16),
            pltpu.VMEM((TILES, TPL_DEV * SKY, 128), jnp.float32),
            pltpu.SemaphoreType.DMA((TILES,)),
        ],
        compiler_params=pltpu.CompilerParams(vmem_limit_bytes=16 * 1024 * 1024),
    )(half, sky_delay, gain_near, gain_far, own, got)
    return out.reshape(TPL_DEV, SKY, HALF)


def solution(mesh):
    return jax.shard_map(
        on_device,
        mesh=mesh,
        in_specs=(P("det", None, "bank"), P("det", "bank"), P("bank"), P("bank"), P(), P(), P()),
        out_specs=P("bank", None, "det"),
        check_vma=False,
    )
```

```python
import functools
import math

import jax
import jax.numpy as jnp
import numpy as np
from jax import lax
from jax.experimental import pallas as pl
from jax.experimental.pallas import tpu as pltpu
from jax.sharding import PartitionSpec as P

DFT_ROWS = 512
DFT_COLS = 256
SAMPLES = 131072
LOW_BIN = 1920
WIN_BLOCKS = 8
WINDOW = 4096
HALF = WINDOW // 2
TPL_DEV = 16
SKY = 16
MASSES = 64
N_Z = 16
N_XY = 16
COLS = WIN_BLOCKS + 2
SPAN = HALF + 128
PAYLOAD = 640
STRIP = 16
BATCH = 8
LAST_ROWS = 24
EARLY = 5
TILES = HALF // 128
GROUP = 4
STAGES = 4
BIG = 60 * 1024 * 1024
FILTER_VMEM = 46 * 1024 * 1024
WAVE_ROOM = 80

MSUN_SEC = 4.925491e-06
SAMPLE_RATE = 2048.0

Z_ORDER = [9, 11, 13, 15, 1, 3, 5, 7, 8, 10, 12, 14, 0, 2, 4, 6]
XY_ORDER = [(k + 10) % N_XY for k in range(N_XY)]


def group_lists():
    z_groups = [[q * N_Z + z for z in Z_ORDER] for q in range(N_XY)]
    xy_groups = [[q * N_Z + z for q in XY_ORDER] for z in range(N_Z)]
    return z_groups, xy_groups


def constant_tables():
    rows = np.array([[q * N_Z + z for z in Z_ORDER] for q in XY_ORDER])
    odd, even = rows[:, :8].reshape(-1), rows[:, 8:].reshape(-1)
    k1 = np.concatenate([odd, even])
    k2 = np.arange(DFT_COLS)
    bins = 256 * k1[None, :] + k2[:, None]
    freq = np.maximum(bins * (SAMPLE_RATE / SAMPLES), 1.0)
    powers = np.stack(
        [
            freq ** (-5.0 / 3.0),
            freq**-1.0,
            freq ** (-2.0 / 3.0),
            np.where(bins >= LOW_BIN, freq ** (-7.0 / 6.0), 0.0),
            freq**4,
        ]
    ).astype(np.float32)

    t1 = np.arange(256)

    def first(rows_k):
        angle = 2.0 * np.pi / 512 * (rows_k[:, None] * t1[None, :] % 512)
        c, s = np.cos(angle), np.sin(angle)
        return np.concatenate([np.concatenate([c, s], 1), np.concatenate([-s, c], 1)], 0)

    first_tables = np.stack([first(odd), first(even)])
    angle = 2.0 * np.pi / SAMPLES * (k2[:, None] * t1[None, :] % SAMPLES)
    twist = np.stack([np.cos(angle), np.sin(angle)]).astype(np.float32)
    t2 = DFT_COLS // 2 - WIN_BLOCKS // 2 - 1 + np.arange(COLS)
    last = np.zeros((2 * LAST_ROWS, 1024))
    for side in range(2):
        steps = k2[None, :] * (t2[:, None] * DFT_ROWS + 256 * side)
        angle = 2.0 * np.pi / SAMPLES * (steps % SAMPLES)
        c, s = np.cos(angle), np.sin(angle)
        rows = np.concatenate([np.concatenate([c, -s], 1), np.concatenate([s, c], 1)], 0)
        at = LAST_ROWS * side
        last[at : at + 2 * COLS] = np.concatenate([-rows if side else rows, rows], 1)

    seconds = 6.0 * 1.03 ** np.arange(MASSES) * MSUN_SEC
    ratio = 0.16 + 0.09 * np.arange(64) / 63.0
    x = np.pi * seconds
    turn = 1.0 / (2.0 * np.pi)
    scalars = np.stack(
        [
            turn * x ** (-5.0 / 3.0),
            turn * x**-1.0,
            turn * x ** (-2.0 / 3.0),
            -((6.0**1.5 * x) ** 4) / math.log(2.0),
            3.0 / (128.0 * ratio),
            3715.0 / 756.0 + 55.0 * ratio / 9.0,
            (113.0 - 76.0 * ratio) / 12.0,
            np.zeros(64),
        ]
    ).astype(np.float32)
    return (
        powers,
        first_tables.astype(jnp.bfloat16),
        twist,
        last.astype(jnp.bfloat16),
        scalars,
    )


def even_fit(function, terms):
    nodes = 0.5 * np.cos(np.pi * (np.arange(400) + 0.5) / 400)
    design = (nodes[:, None] ** 2) ** np.arange(terms)[None, :]
    fitted = np.linalg.lstsq(design, function(nodes), rcond=None)[0]
    return [float(np.float32(v)) for v in fitted]


ROOT2 = math.sqrt(2.0)
SIN_FIT = even_fit(lambda r: ROOT2 * np.pi * np.sinc(r), 5)
ROUND_SHIFT = 12582912.0


def horner(coefs, square):
    total = coefs[-1] * square + coefs[-2]
    for c in coefs[-3::-1]:
        total = total * square + c
    return total


def payload_row(bank, strain, asd):
    weight = asd * asd
    over = strain * weight
    bin_id = bank * 256 + lax.broadcasted_iota(jnp.int32, (1, 256), 1)
    clipped = jnp.maximum(bin_id.astype(jnp.float32) * (SAMPLE_RATE / SAMPLES), 1.0)
    square = clipped * clipped
    falling = jnp.exp((-7.0 / 3.0) * jnp.log(clipped))
    weighted = jnp.where(bin_id >= LOW_BIN, falling, 0.0) * weight
    mass_id = lax.broadcasted_iota(jnp.int32, (MASSES, 1), 0).astype(jnp.float32)
    start = math.log(2.0) + 4.0 * math.log(6.0**1.5 * math.pi * 6.0 * MSUN_SEC)
    steep = jnp.exp(4.0 * math.log(1.03) * mass_id + start)
    column = jnp.sum(jnp.exp(-steep * (square * square)) * weighted, axis=1, keepdims=True)
    row_id = lax.broadcasted_iota(jnp.int32, (MASSES, MASSES), 0)
    col_id = lax.broadcasted_iota(jnp.int32, (MASSES, MASSES), 1)
    norms = jnp.sum(jnp.where(row_id == col_id, column, 0.0), axis=0, keepdims=True)
    coarse = norms.astype(jnp.bfloat16).astype(jnp.float32)
    return jnp.concatenate([over[0:1], over[1:2], coarse, norms - coarse], axis=1)


def slot_scalars(slot, indices_ref, scalars_ref):
    entry = indices_ref[slot]
    mass, eta = entry % 64, entry // 64 % 64
    spin = -0.6 + 0.4 * (entry // 4096).astype(jnp.float32)
    lead = scalars_ref[4, eta]
    c53 = lead * scalars_ref[0, mass]
    c1 = lead * scalars_ref[5, eta] * scalars_ref[1, mass]
    c23 = lead * (4.0 * spin * scalars_ref[6, eta] - 16.0 * math.pi) * scalars_ref[2, mass]
    return c53, c1, c23, scalars_ref[3, mass]


def wave(coefs, powers, here):
    c53, c1, c23, steep = coefs
    turns = (
        c53 * powers[0, here, :] + c1 * powers[1, here, :] + (c23 * powers[2, here, :] - 0.125)
    )
    rest = turns - ((turns + ROUND_SHIFT) - ROUND_SHIFT)
    square = rest * rest
    half_sin = horner(SIN_FIT, square) * rest
    cosine = 1.0 - half_sin * half_sin
    above = jnp.maximum(1.0 + cosine, 1e-12)
    half_cos = above * lax.rsqrt(above)
    envelope = powers[3, here, :] * jnp.exp2(steep * powers[4, here, :])
    return envelope * cosine, envelope * (half_sin * half_cos)


def early_slots(bank, count):
    z = bank % N_Z
    early = jnp.where(z < 4, EARLY, jnp.where(z < 7, EARLY // 2, 0))
    return jnp.minimum(early, rounded_up(count))


def wave_kernel(
    bank_ref,
    indices_ref,
    counts_ref,
    scalars_ref,
    powers_hbm,
    early_ref,
    waves_ref,
    powers,
    staged,
    sems,
):
    first, last = early_slots(bank_ref[0], counts_ref[0]), rounded_up(counts_ref[0])
    write_waves(first, last, indices_ref, scalars_ref, powers_hbm, waves_ref, powers, staged, sems)


def write_waves(first, last, indices_ref, scalars_ref, powers_hbm, waves_ref, powers, staged, sems):
    def store(slot):
        place = slot % STAGES
        return pltpu.make_async_copy(staged.at[place], waves_ref.at[slot], sems.at[place])

    def load(strip):
        rows = pl.ds(strip * 64, 64)
        return pltpu.make_async_copy(
            powers_hbm.at[:, rows], powers.at[:, rows], sems.at[STAGES + strip]
        )

    @pl.when(last > first)
    def _():
        for strip in range(4):
            load(strip).start()

    @pl.loop(first, last)
    def _(slot):
        coefs = slot_scalars(slot, indices_ref, scalars_ref)

        @pl.when(slot >= first + STAGES)
        def _():
            store(slot - STAGES).wait()

        @pl.loop(0, DFT_COLS // 64)
        def _(strip):
            @pl.when(slot == first)
            def _():
                load(strip).wait()

            for piece in range(4):
                here = pl.ds(pl.multiple_of(strip * 64 + piece * 16, 16), 16)
                cosine, sine = wave(coefs, powers, here)
                staged[slot % STAGES, 0, here, :] = cosine.astype(jnp.bfloat16)
                staged[slot % STAGES, 1, here, :] = sine.astype(jnp.bfloat16)

        store(slot).start()

    for back in range(STAGES, 0, -1):

        @pl.when(last - first >= back)
        def _():
            store(last - back).wait()


def rounded_up(count):
    return (count + BATCH - 1) // BATCH * BATCH


def prepare_kernel(
    bank_ref,
    indices_ref,
    counts_ref,
    scalars_ref,
    strain_ref,
    asd_ref,
    powers_hbm,
    out_ref,
    waves_ref,
    powers,
    staged,
    sems,
):
    row = payload_row(bank_ref[0], strain_ref[...], asd_ref[...])
    pair = jnp.concatenate([row[:, : PAYLOAD // 2], row[:, PAYLOAD // 2 :]], axis=0)
    out_ref[...] = jnp.broadcast_to(pair.astype(jnp.bfloat16)[None], out_ref.shape)
    last = early_slots(bank_ref[0], counts_ref[0])
    write_waves(0, last, indices_ref, scalars_ref, powers_hbm, waves_ref, powers, staged, sems)


def filter_kernel(
    indices_ref,
    counts_ref,
    half_ref,
    gathered_ref,
    first_ref,
    twist_ref,
    last_ref,
    waves_ref,
    own_ref,
    send_ref,
    spectrum,
    products,
    middle,
    twisted,
    series,
    waves,
    sems,
):
    count = counts_ref[0]
    slots = rounded_up(count)

    def fetch(slot):
        place = slot % (2 * BATCH)
        return pltpu.make_async_copy(waves_ref.at[slot], waves.at[place], sems.at[place])

    def fetch_batch(batch):
        for place in range(BATCH):
            fetch(batch * BATCH + place).start()

    fetch_batch(0)

    for part in range(2):
        block = gathered_ref[:, :, 256 * part : 256 * part + 256].astype(jnp.float32)
        for parity in range(2):
            rows = block[:, 8 * parity : 8 * parity + 8].reshape(128, 256)
            spectrum[part, :, 128 * parity : 128 * parity + 128] = rows.T
    sums = jnp.sum(
        gathered_ref[:, :, 512:640].astype(jnp.float32).reshape(256, 128), axis=0, keepdims=True
    )
    norm_row = sums[:, :MASSES] + sums[:, MASSES:]
    lane_id = lax.broadcasted_iota(jnp.int32, (1, MASSES), 1)
    series[...] = jnp.zeros_like(series)

    def multiply(slot, place):
        buffer = slot % (2 * BATCH)
        fetch(slot).wait()
        for i in range(0, DFT_COLS, STRIP):
            here, there = slice(i, i + STRIP), slice(256 * place + i, 256 * place + i + STRIP)
            cosine = waves[buffer, 0, here, :].astype(jnp.float32)
            sine = waves[buffer, 1, here, :].astype(jnp.float32)
            re, im = spectrum[0, here, :], spectrum[1, here, :]
            real_part = (re * cosine - im * sine).astype(jnp.bfloat16)
            imag_part = (re * sine + im * cosine).astype(jnp.bfloat16)
            for parity in range(2):
                lanes = slice(128 * parity, 128 * parity + 128)
                products[parity, there, 0:128] = real_part[:, lanes]
                products[parity, there, 128:256] = imag_part[:, lanes]

    def twist(place, parity):
        for i in range(0, DFT_COLS, STRIP):
            here = slice(i, i + STRIP)
            there = slice(256 * place + i, 256 * place + i + STRIP)
            upper, lower = middle[parity, there, 0:256], middle[parity, there, 256:512]
            c, s = twist_ref[0, here, :], twist_ref[1, here, :]
            at = 512 * parity + i
            twisted[place, at : at + STRIP] = (upper * c - lower * s).astype(jnp.bfloat16)
            twisted[place, at + 256 : at + 256 + STRIP] = (upper * s + lower * c).astype(
                jnp.bfloat16
            )

    def finish(slot, place):
        mass = indices_ref[slot] % 64
        norm = jnp.sum(jnp.where(lane_id == mass, norm_row, 0.0), axis=1, keepdims=True)
        scale = lax.rsqrt(norm) * jnp.where(slot < count, 1.0, 0.0)
        result = scale * jnp.dot(
            last_ref[...], twisted[place], preferred_element_type=jnp.float32
        )
        for side in range(2):
            rows = slice(LAST_ROWS * side, LAST_ROWS * side + 2 * COLS)
            for i in range(2):
                series[2 * side + i, pl.ds(slot, 2 * COLS, stride=TPL_DEV), :] = result[
                    rows, 128 * i : 128 * i + 128
                ]

    @pl.loop(0, slots // BATCH)
    def _(batch):
        @pl.when((batch + 1) * BATCH < slots)
        def _():
            fetch_batch(batch + 1)

        for place in range(BATCH):
            multiply(batch * BATCH + place, place)
        for parity in range(2):
            middle[parity] = jnp.dot(
                products[parity], first_ref[parity], preferred_element_type=jnp.float32
            )
        for parity in range(2):
            for place in range(BATCH):
                twist(place, parity)
        for place in range(BATCH):
            finish(batch * BATCH + place, place)

    def write(out_ref, half, shifted):
        def tile_of(part, index):
            column, tile = divmod(index, 4)
            start = (part * COLS + 4 * half + column) * TPL_DEV
            return series[tile, pl.ds(pl.multiple_of(start, TPL_DEV), TPL_DEV), :]

        lower = lax.broadcasted_iota(jnp.int32, (TPL_DEV, 128), 1) < 64
        for part in range(2):
            before = None
            for i in range(SPAN // 128):
                tile = tile_of(part, 4 + i)
                if shifted:
                    if before is None:
                        before = pltpu.roll(tile_of(part, 3), 64, axis=1)
                    turned = pltpu.roll(tile, 64, axis=1)
                    tile, before = jnp.where(lower, before, turned), turned
                out_ref[part, :, 128 * i : 128 * i + 128] = tile.astype(jnp.bfloat16)

    for det in range(2):

        @pl.when(half_ref[0] == det)
        def _():
            write(own_ref, det, det == 1)
            write(send_ref, 1 - det, det == 1)


def coherent_kernel(
    half_ref,
    delay_ref,
    near_gain_ref,
    far_gain_ref,
    own_ref,
    got_ref,
    out_ref,
    near,
    pairs,
    picks,
    tiles,
    sems,
):
    def unpack(near_ref, far_ref):
        for tile in range(TILES):
            for part in range(2):
                rows = slice(32 * tile + 16 * part, 32 * tile + 16 * part + 16)
                near[rows, :] = near_ref[part, :, 128 * tile : 128 * tile + 128].astype(jnp.float32)
                pairs[rows, :] = far_ref[part, :, 128 * tile : 128 * tile + 256]

    @pl.when(half_ref[0] == 0)
    def _():
        unpack(own_ref, got_ref.at[1])

    @pl.when(half_ref[0] == 1)
    def _():
        unpack(got_ref.at[0], own_ref)

    row_id = lax.broadcasted_iota(jnp.int32, (256, 256), 0)
    col_id = lax.broadcasted_iota(jnp.int32, (256, 256), 1)

    def copy_out(tile):
        lanes = slice(128 * tile, 128 * tile + 128)
        return pltpu.make_async_copy(tiles.at[tile], out_ref.at[:, lanes], sems.at[tile])

    for group in range(0, TILES, GROUP):
        for sky in range(0, SKY, 2):
            if group == 0:
                shift = jnp.where(col_id < 128, delay_ref[sky] + 64, delay_ref[sky + 1] - 64)
                picks[sky // 2] = jnp.where(row_id == col_id + shift, 1.0, 0.0).astype(jnp.bfloat16)
            delayed = jnp.dot(
                pairs[32 * group : 32 * (group + GROUP), :],
                picks[sky // 2],
                preferred_element_type=jnp.float32,
            )
            for side in range(2):
                gain_near, gain_far = near_gain_ref[sky + side], far_gain_ref[sky + side]
                power = gain_near * gain_near + gain_far * gain_far
                inverse = lax.rsqrt(jnp.full((1, 128), power, jnp.float32))
                near_row = jnp.broadcast_to(gain_near * inverse, (TPL_DEV, 128))
                far_row = jnp.broadcast_to(gain_far * inverse, (TPL_DEV, 128))
                lanes = slice(128 * side, 128 * side + 128)
                for i in range(GROUP):
                    tile = group + i
                    re, im = (
                        near_row * near[32 * tile + at : 32 * tile + at + 16, :]
                        + far_row * delayed[32 * i + at : 32 * i + at + 16, lanes]
                        for at in (0, 16)
                    )
                    place = pl.ds(sky + side, TPL_DEV, stride=SKY)
                    tiles[tile, place, :] = re * re + im * im
        for i in range(GROUP):
            copy_out(group + i).start()

    for tile in range(TILES):
        copy_out(tile).wait()


ANY = pl.BlockSpec(memory_space=pl.ANY)
VMEM = pl.BlockSpec(memory_space=pltpu.VMEM)
SMEM = pl.BlockSpec(memory_space=pltpu.SMEM)


def on_device(strain, asd_inv, indices, counts, sky_delay, gain_near, gain_far):
    powers, first_tables, twist, last, scalars = constant_tables()
    z_groups, xy_groups = group_lists()
    bank = lax.axis_index("bank").astype(jnp.int32)[None]
    half = lax.axis_index("det").astype(jnp.int32)[None]
    room = jax.ShapeDtypeStruct((WAVE_ROOM, 2, DFT_COLS, 256), jnp.bfloat16)
    wave_scratch = [
        pltpu.VMEM((5, DFT_COLS, 256), jnp.float32),
        pltpu.VMEM((STAGES, 2, DFT_COLS, 256), jnp.bfloat16),
        pltpu.SemaphoreType.DMA((STAGES + 4,)),
    ]
    payload, early = pl.pallas_call(
        prepare_kernel,
        out_shape=(jax.ShapeDtypeStruct((N_Z, 2, PAYLOAD // 2), jnp.bfloat16), room),
        in_specs=[SMEM] * 4 + [VMEM] * 2 + [ANY],
        out_specs=(VMEM, ANY),
        scratch_shapes=wave_scratch,
        compiler_params=pltpu.CompilerParams(vmem_limit_bytes=BIG),
    )(bank, indices, counts, scalars, strain[0], asd_inv, powers)
    line = lax.all_to_all(payload, "bank", 0, 0, axis_index_groups=z_groups)
    spread = jnp.broadcast_to(line.reshape(1, N_Z, PAYLOAD), (N_XY, N_Z, PAYLOAD))
    plane = lax.all_to_all(spread, "bank", 0, 0, axis_index_groups=xy_groups)
    waves = pl.pallas_call(
        wave_kernel,
        out_shape=room,
        in_specs=[SMEM] * 4 + [ANY] * 2,
        out_specs=ANY,
        scratch_shapes=wave_scratch,
        input_output_aliases={5: 0},
        cost_estimate=pl.CostEstimate(
            flops=40 * 2**20, bytes_accessed=10 * 2**20, transcendentals=2**20
        ),
        compiler_params=pltpu.CompilerParams(vmem_limit_bytes=BIG),
    )(bank, indices, counts, scalars, powers, early)
    window = jax.ShapeDtypeStruct((2, TPL_DEV, SPAN), jnp.bfloat16)
    own, send = pl.pallas_call(
        filter_kernel,
        out_shape=(window, window),
        in_specs=[SMEM] * 3 + [VMEM] * 4 + [ANY],
        out_specs=(VMEM, VMEM),
        scratch_shapes=[
            pltpu.VMEM((2, DFT_COLS, 256), jnp.float32),
            pltpu.VMEM((2, BATCH * DFT_COLS, 256), jnp.bfloat16),
            pltpu.VMEM((2, BATCH * DFT_COLS, 512), jnp.float32),
            pltpu.VMEM((BATCH, 1024, 256), jnp.bfloat16),
            pltpu.VMEM((4, 2 * COLS * TPL_DEV, 128), jnp.float32),
            pltpu.VMEM((2 * BATCH, 2, DFT_COLS, 256), jnp.bfloat16),
            pltpu.SemaphoreType.DMA((2 * BATCH,)),
        ],
        compiler_params=pltpu.CompilerParams(vmem_limit_bytes=FILTER_VMEM),
    )(indices, counts, half, plane, first_tables, twist, last, waves)
    got = lax.all_gather(send, "det", axis=0)
    out = pl.pallas_call(
        coherent_kernel,
        out_shape=jax.ShapeDtypeStruct((TPL_DEV * SKY, HALF), jnp.float32),
        in_specs=[SMEM] * 4 + [VMEM] * 2,
        out_specs=pl.BlockSpec(memory_space=pl.ANY),
        scratch_shapes=[
            pltpu.VMEM((2 * TPL_DEV * TILES, 128), jnp.float32),
            pltpu.VMEM((2 * TPL_DEV * TILES, 256), jnp.bfloat16),
            pltpu.VMEM((SKY // 2, 256, 256), jnp.bfloat16),
            pltpu.VMEM((TILES, TPL_DEV * SKY, 128), jnp.float32),
            pltpu.SemaphoreType.DMA((TILES,)),
        ],
        compiler_params=pltpu.CompilerParams(vmem_limit_bytes=16 * 1024 * 1024),
    )(half, sky_delay, gain_near, gain_far, own, got)
    return out.reshape(TPL_DEV, SKY, HALF)


def solution(mesh):
    return jax.shard_map(
        on_device,
        mesh=mesh,
        in_specs=(P("det", None, "bank"), P("det", "bank"), P("bank"), P("bank"), P(), P(), P()),
        out_specs=P("bank", None, "det"),
        check_vma=False,
    )
```

```python
import functools
import math

import jax
import jax.numpy as jnp
import numpy as np
from jax import lax
from jax.experimental import pallas as pl
from jax.experimental.pallas import tpu as pltpu
from jax.sharding import PartitionSpec as P

DFT_ROWS = 512
DFT_COLS = 256
SAMPLES = 131072
LOW_BIN = 1920
WIN_BLOCKS = 8
WINDOW = 4096
HALF = WINDOW // 2
TPL_DEV = 16
SKY = 16
MASSES = 64
N_Z = 16
N_XY = 16
COLS = WIN_BLOCKS + 2
SPAN = HALF + 128
PAYLOAD = 640
STRIP = 16
BATCH = 8
LAST_ROWS = 24
EARLY = 5
TILES = HALF // 128
GROUP = 4
STAGES = 4
BIG = 60 * 1024 * 1024
FILTER_VMEM = 46 * 1024 * 1024
WAVE_ROOM = 80

MSUN_SEC = 4.925491e-06
SAMPLE_RATE = 2048.0

Z_ORDER = [9, 11, 13, 15, 1, 3, 5, 7, 8, 10, 12, 14, 0, 2, 4, 6]
XY_ORDER = [(k + 5) % N_XY for k in range(N_XY)]


def group_lists():
    z_groups = [[q * N_Z + z for z in Z_ORDER] for q in range(N_XY)]
    xy_groups = [[q * N_Z + z for q in XY_ORDER] for z in range(N_Z)]
    return z_groups, xy_groups


def constant_tables():
    rows = np.array([[q * N_Z + z for z in Z_ORDER] for q in XY_ORDER])
    odd, even = rows[:, :8].reshape(-1), rows[:, 8:].reshape(-1)
    k1 = np.concatenate([odd, even])
    k2 = np.arange(DFT_COLS)
    bins = 256 * k1[None, :] + k2[:, None]
    freq = np.maximum(bins * (SAMPLE_RATE / SAMPLES), 1.0)
    powers = np.stack(
        [
            freq ** (-5.0 / 3.0),
            freq**-1.0,
            freq ** (-2.0 / 3.0),
            np.where(bins >= LOW_BIN, freq ** (-7.0 / 6.0), 0.0),
            freq**4,
        ]
    ).astype(np.float32)

    t1 = np.arange(256)

    def first(rows_k):
        angle = 2.0 * np.pi / 512 * (rows_k[:, None] * t1[None, :] % 512)
        c, s = np.cos(angle), np.sin(angle)
        return np.concatenate([np.concatenate([c, s], 1), np.concatenate([-s, c], 1)], 0)

    first_tables = np.stack([first(odd), first(even)])
    angle = 2.0 * np.pi / SAMPLES * (k2[:, None] * t1[None, :] % SAMPLES)
    twist = np.stack([np.cos(angle), np.sin(angle)]).astype(np.float32)
    t2 = DFT_COLS // 2 - WIN_BLOCKS // 2 - 1 + np.arange(COLS)
    last = np.zeros((2 * LAST_ROWS, 1024))
    for side in range(2):
        steps = k2[None, :] * (t2[:, None] * DFT_ROWS + 256 * side)
        angle = 2.0 * np.pi / SAMPLES * (steps % SAMPLES)
        c, s = np.cos(angle), np.sin(angle)
        rows = np.concatenate([np.concatenate([c, -s], 1), np.concatenate([s, c], 1)], 0)
        at = LAST_ROWS * side
        last[at : at + 2 * COLS] = np.concatenate([-rows if side else rows, rows], 1)

    seconds = 6.0 * 1.03 ** np.arange(MASSES) * MSUN_SEC
    ratio = 0.16 + 0.09 * np.arange(64) / 63.0
    x = np.pi * seconds
    turn = 1.0 / (2.0 * np.pi)
    scalars = np.stack(
        [
            turn * x ** (-5.0 / 3.0),
            turn * x**-1.0,
            turn * x ** (-2.0 / 3.0),
            -((6.0**1.5 * x) ** 4) / math.log(2.0),
            3.0 / (128.0 * ratio),
            3715.0 / 756.0 + 55.0 * ratio / 9.0,
            (113.0 - 76.0 * ratio) / 12.0,
            np.zeros(64),
        ]
    ).astype(np.float32)
    return (
        powers,
        first_tables.astype(jnp.bfloat16),
        twist,
        last.astype(jnp.bfloat16),
        scalars,
    )


def even_fit(function, terms):
    nodes = 0.5 * np.cos(np.pi * (np.arange(400) + 0.5) / 400)
    design = (nodes[:, None] ** 2) ** np.arange(terms)[None, :]
    fitted = np.linalg.lstsq(design, function(nodes), rcond=None)[0]
    return [float(np.float32(v)) for v in fitted]


ROOT2 = math.sqrt(2.0)
SIN_FIT = even_fit(lambda r: ROOT2 * np.pi * np.sinc(r), 5)
ROUND_SHIFT = 12582912.0


def horner(coefs, square):
    total = coefs[-1] * square + coefs[-2]
    for c in coefs[-3::-1]:
        total = total * square + c
    return total


def payload_row(bank, strain, asd):
    weight = asd * asd
    over = strain * weight
    bin_id = bank * 256 + lax.broadcasted_iota(jnp.int32, (1, 256), 1)
    clipped = jnp.maximum(bin_id.astype(jnp.float32) * (SAMPLE_RATE / SAMPLES), 1.0)
    square = clipped * clipped
    falling = jnp.exp((-7.0 / 3.0) * jnp.log(clipped))
    weighted = jnp.where(bin_id >= LOW_BIN, falling, 0.0) * weight
    mass_id = lax.broadcasted_iota(jnp.int32, (MASSES, 1), 0).astype(jnp.float32)
    start = math.log(2.0) + 4.0 * math.log(6.0**1.5 * math.pi * 6.0 * MSUN_SEC)
    steep = jnp.exp(4.0 * math.log(1.03) * mass_id + start)
    column = jnp.sum(jnp.exp(-steep * (square * square)) * weighted, axis=1, keepdims=True)
    row_id = lax.broadcasted_iota(jnp.int32, (MASSES, MASSES), 0)
    col_id = lax.broadcasted_iota(jnp.int32, (MASSES, MASSES), 1)
    norms = jnp.sum(jnp.where(row_id == col_id, column, 0.0), axis=0, keepdims=True)
    coarse = norms.astype(jnp.bfloat16).astype(jnp.float32)
    return jnp.concatenate([over[0:1], over[1:2], coarse, norms - coarse], axis=1)


def slot_scalars(slot, indices_ref, scalars_ref):
    entry = indices_ref[slot]
    mass, eta = entry % 64, entry // 64 % 64
    spin = -0.6 + 0.4 * (entry // 4096).astype(jnp.float32)
    lead = scalars_ref[4, eta]
    c53 = lead * scalars_ref[0, mass]
    c1 = lead * scalars_ref[5, eta] * scalars_ref[1, mass]
    c23 = lead * (4.0 * spin * scalars_ref[6, eta] - 16.0 * math.pi) * scalars_ref[2, mass]
    return c53, c1, c23, scalars_ref[3, mass]


def wave(coefs, powers, here):
    c53, c1, c23, steep = coefs
    turns = (
        c53 * powers[0, here, :] + c1 * powers[1, here, :] + (c23 * powers[2, here, :] - 0.125)
    )
    rest = turns - ((turns + ROUND_SHIFT) - ROUND_SHIFT)
    square = rest * rest
    half_sin = horner(SIN_FIT, square) * rest
    cosine = 1.0 - half_sin * half_sin
    above = jnp.maximum(1.0 + cosine, 1e-12)
    half_cos = above * lax.rsqrt(above)
    envelope = powers[3, here, :] * jnp.exp2(steep * powers[4, here, :])
    return envelope * cosine, envelope * (half_sin * half_cos)


def early_slots(bank, count):
    z = bank % N_Z
    early = jnp.where(z < 4, EARLY, jnp.where(z < 7, EARLY // 2, 0))
    return jnp.minimum(early, rounded_up(count))


def wave_kernel(
    bank_ref,
    indices_ref,
    counts_ref,
    scalars_ref,
    powers_hbm,
    early_ref,
    waves_ref,
    powers,
    staged,
    sems,
):
    first, last = early_slots(bank_ref[0], counts_ref[0]), rounded_up(counts_ref[0])
    write_waves(first, last, indices_ref, scalars_ref, powers_hbm, waves_ref, powers, staged, sems)


def write_waves(first, last, indices_ref, scalars_ref, powers_hbm, waves_ref, powers, staged, sems):
    def store(slot):
        place = slot % STAGES
        return pltpu.make_async_copy(staged.at[place], waves_ref.at[slot], sems.at[place])

    def load(strip):
        rows = pl.ds(strip * 64, 64)
        return pltpu.make_async_copy(
            powers_hbm.at[:, rows], powers.at[:, rows], sems.at[STAGES + strip]
        )

    @pl.when(last > first)
    def _():
        for strip in range(4):
            load(strip).start()

    @pl.loop(first, last)
    def _(slot):
        coefs = slot_scalars(slot, indices_ref, scalars_ref)

        @pl.when(slot >= first + STAGES)
        def _():
            store(slot - STAGES).wait()

        @pl.loop(0, DFT_COLS // 64)
        def _(strip):
            @pl.when(slot == first)
            def _():
                load(strip).wait()

            for piece in range(4):
                here = pl.ds(pl.multiple_of(strip * 64 + piece * 16, 16), 16)
                cosine, sine = wave(coefs, powers, here)
                staged[slot % STAGES, 0, here, :] = cosine.astype(jnp.bfloat16)
                staged[slot % STAGES, 1, here, :] = sine.astype(jnp.bfloat16)

        store(slot).start()

    for back in range(STAGES, 0, -1):

        @pl.when(last - first >= back)
        def _():
            store(last - back).wait()


def rounded_up(count):
    return (count + BATCH - 1) // BATCH * BATCH


def prepare_kernel(
    bank_ref,
    indices_ref,
    counts_ref,
    scalars_ref,
    strain_ref,
    asd_ref,
    powers_hbm,
    out_ref,
    waves_ref,
    powers,
    staged,
    sems,
):
    row = payload_row(bank_ref[0], strain_ref[...], asd_ref[...])
    pair = jnp.concatenate([row[:, : PAYLOAD // 2], row[:, PAYLOAD // 2 :]], axis=0)
    out_ref[...] = jnp.broadcast_to(pair.astype(jnp.bfloat16)[None], out_ref.shape)
    last = early_slots(bank_ref[0], counts_ref[0])
    write_waves(0, last, indices_ref, scalars_ref, powers_hbm, waves_ref, powers, staged, sems)


def filter_kernel(
    indices_ref,
    counts_ref,
    half_ref,
    gathered_ref,
    first_ref,
    twist_ref,
    last_ref,
    waves_ref,
    own_ref,
    send_ref,
    spectrum,
    products,
    middle,
    twisted,
    series,
    waves,
    sems,
):
    count = counts_ref[0]
    slots = rounded_up(count)

    def fetch(slot):
        place = slot % (2 * BATCH)
        return pltpu.make_async_copy(waves_ref.at[slot], waves.at[place], sems.at[place])

    def fetch_batch(batch):
        for place in range(BATCH):
            fetch(batch * BATCH + place).start()

    fetch_batch(0)

    for part in range(2):
        block = gathered_ref[:, :, 256 * part : 256 * part + 256].astype(jnp.float32)
        for parity in range(2):
            rows = block[:, 8 * parity : 8 * parity + 8].reshape(128, 256)
            spectrum[part, :, 128 * parity : 128 * parity + 128] = rows.T
    sums = jnp.sum(
        gathered_ref[:, :, 512:640].astype(jnp.float32).reshape(256, 128), axis=0, keepdims=True
    )
    norm_row = sums[:, :MASSES] + sums[:, MASSES:]
    lane_id = lax.broadcasted_iota(jnp.int32, (1, MASSES), 1)
    series[...] = jnp.zeros_like(series)

    def multiply(slot, place):
        buffer = slot % (2 * BATCH)
        fetch(slot).wait()
        for i in range(0, DFT_COLS, STRIP):
            here, there = slice(i, i + STRIP), slice(256 * place + i, 256 * place + i + STRIP)
            cosine = waves[buffer, 0, here, :].astype(jnp.float32)
            sine = waves[buffer, 1, here, :].astype(jnp.float32)
            re, im = spectrum[0, here, :], spectrum[1, here, :]
            real_part = (re * cosine - im * sine).astype(jnp.bfloat16)
            imag_part = (re * sine + im * cosine).astype(jnp.bfloat16)
            for parity in range(2):
                lanes = slice(128 * parity, 128 * parity + 128)
                products[parity, there, 0:128] = real_part[:, lanes]
                products[parity, there, 128:256] = imag_part[:, lanes]

    def twist(place, parity):
        for i in range(0, DFT_COLS, STRIP):
            here = slice(i, i + STRIP)
            there = slice(256 * place + i, 256 * place + i + STRIP)
            upper, lower = middle[parity, there, 0:256], middle[parity, there, 256:512]
            c, s = twist_ref[0, here, :], twist_ref[1, here, :]
            at = 512 * parity + i
            twisted[place, at : at + STRIP] = (upper * c - lower * s).astype(jnp.bfloat16)
            twisted[place, at + 256 : at + 256 + STRIP] = (upper * s + lower * c).astype(
                jnp.bfloat16
            )

    def finish(slot, place):
        mass = indices_ref[slot] % 64
        norm = jnp.sum(jnp.where(lane_id == mass, norm_row, 0.0), axis=1, keepdims=True)
        scale = lax.rsqrt(norm) * jnp.where(slot < count, 1.0, 0.0)
        result = scale * jnp.dot(
            last_ref[...], twisted[place], preferred_element_type=jnp.float32
        )
        for side in range(2):
            rows = slice(LAST_ROWS * side, LAST_ROWS * side + 2 * COLS)
            for i in range(2):
                series[2 * side + i, pl.ds(slot, 2 * COLS, stride=TPL_DEV), :] = result[
                    rows, 128 * i : 128 * i + 128
                ]

    @pl.loop(0, slots // BATCH)
    def _(batch):
        @pl.when((batch + 1) * BATCH < slots)
        def _():
            fetch_batch(batch + 1)

        for place in range(BATCH):
            multiply(batch * BATCH + place, place)
        for parity in range(2):
            middle[parity] = jnp.dot(
                products[parity], first_ref[parity], preferred_element_type=jnp.float32
            )
        for parity in range(2):
            for place in range(BATCH):
                twist(place, parity)
        for place in range(BATCH):
            finish(batch * BATCH + place, place)

    def write(out_ref, half, shifted):
        def tile_of(part, index):
            column, tile = divmod(index, 4)
            start = (part * COLS + 4 * half + column) * TPL_DEV
            return series[tile, pl.ds(pl.multiple_of(start, TPL_DEV), TPL_DEV), :]

        lower = lax.broadcasted_iota(jnp.int32, (TPL_DEV, 128), 1) < 64
        for part in range(2):
            before = None
            for i in range(SPAN // 128):
                tile = tile_of(part, 4 + i)
                if shifted:
                    if before is None:
                        before = pltpu.roll(tile_of(part, 3), 64, axis=1)
                    turned = pltpu.roll(tile, 64, axis=1)
                    tile, before = jnp.where(lower, before, turned), turned
                out_ref[part, :, 128 * i : 128 * i + 128] = tile.astype(jnp.bfloat16)

    for det in range(2):

        @pl.when(half_ref[0] == det)
        def _():
            write(own_ref, det, det == 1)
            write(send_ref, 1 - det, det == 1)


def coherent_kernel(
    half_ref,
    delay_ref,
    near_gain_ref,
    far_gain_ref,
    own_ref,
    got_ref,
    out_ref,
    near,
    pairs,
    picks,
    tiles,
    sems,
):
    def unpack(near_ref, far_ref):
        for tile in range(TILES):
            for part in range(2):
                rows = slice(32 * tile + 16 * part, 32 * tile + 16 * part + 16)
                near[rows, :] = near_ref[part, :, 128 * tile : 128 * tile + 128].astype(jnp.float32)
                pairs[rows, :] = far_ref[part, :, 128 * tile : 128 * tile + 256]

    @pl.when(half_ref[0] == 0)
    def _():
        unpack(own_ref, got_ref.at[1])

    @pl.when(half_ref[0] == 1)
    def _():
        unpack(got_ref.at[0], own_ref)

    row_id = lax.broadcasted_iota(jnp.int32, (256, 256), 0)
    col_id = lax.broadcasted_iota(jnp.int32, (256, 256), 1)

    def copy_out(tile):
        lanes = slice(128 * tile, 128 * tile + 128)
        return pltpu.make_async_copy(tiles.at[tile], out_ref.at[:, lanes], sems.at[tile])

    for group in range(0, TILES, GROUP):
        for sky in range(0, SKY, 2):
            if group == 0:
                shift = jnp.where(col_id < 128, delay_ref[sky] + 64, delay_ref[sky + 1] - 64)
                picks[sky // 2] = jnp.where(row_id == col_id + shift, 1.0, 0.0).astype(jnp.bfloat16)
            delayed = jnp.dot(
                pairs[32 * group : 32 * (group + GROUP), :],
                picks[sky // 2],
                preferred_element_type=jnp.float32,
            )
            for side in range(2):
                gain_near, gain_far = near_gain_ref[sky + side], far_gain_ref[sky + side]
                power = gain_near * gain_near + gain_far * gain_far
                inverse = lax.rsqrt(jnp.full((1, 128), power, jnp.float32))
                near_row = jnp.broadcast_to(gain_near * inverse, (TPL_DEV, 128))
                far_row = jnp.broadcast_to(gain_far * inverse, (TPL_DEV, 128))
                lanes = slice(128 * side, 128 * side + 128)
                for i in range(GROUP):
                    tile = group + i
                    re, im = (
                        near_row * near[32 * tile + at : 32 * tile + at + 16, :]
                        + far_row * delayed[32 * i + at : 32 * i + at + 16, lanes]
                        for at in (0, 16)
                    )
                    place = pl.ds(sky + side, TPL_DEV, stride=SKY)
                    tiles[tile, place, :] = re * re + im * im
        for i in range(GROUP):
            copy_out(group + i).start()

    for tile in range(TILES):
        copy_out(tile).wait()


ANY = pl.BlockSpec(memory_space=pl.ANY)
VMEM = pl.BlockSpec(memory_space=pltpu.VMEM)
SMEM = pl.BlockSpec(memory_space=pltpu.SMEM)


def on_device(strain, asd_inv, indices, counts, sky_delay, gain_near, gain_far):
    powers, first_tables, twist, last, scalars = constant_tables()
    z_groups, xy_groups = group_lists()
    bank = lax.axis_index("bank").astype(jnp.int32)[None]
    half = lax.axis_index("det").astype(jnp.int32)[None]
    room = jax.ShapeDtypeStruct((WAVE_ROOM, 2, DFT_COLS, 256), jnp.bfloat16)
    wave_scratch = [
        pltpu.VMEM((5, DFT_COLS, 256), jnp.float32),
        pltpu.VMEM((STAGES, 2, DFT_COLS, 256), jnp.bfloat16),
        pltpu.SemaphoreType.DMA((STAGES + 4,)),
    ]
    payload, early = pl.pallas_call(
        prepare_kernel,
        out_shape=(jax.ShapeDtypeStruct((N_Z, 2, PAYLOAD // 2), jnp.bfloat16), room),
        in_specs=[SMEM] * 4 + [VMEM] * 2 + [ANY],
        out_specs=(VMEM, ANY),
        scratch_shapes=wave_scratch,
        compiler_params=pltpu.CompilerParams(vmem_limit_bytes=BIG),
    )(bank, indices, counts, scalars, strain[0], asd_inv, powers)
    line = lax.all_to_all(payload, "bank", 0, 0, axis_index_groups=z_groups)
    spread = jnp.broadcast_to(line.reshape(1, N_Z, PAYLOAD), (N_XY, N_Z, PAYLOAD))
    plane = lax.all_to_all(spread, "bank", 0, 0, axis_index_groups=xy_groups)
    waves = pl.pallas_call(
        wave_kernel,
        out_shape=room,
        in_specs=[SMEM] * 4 + [ANY] * 2,
        out_specs=ANY,
        scratch_shapes=wave_scratch,
        input_output_aliases={5: 0},
        cost_estimate=pl.CostEstimate(
            flops=40 * 2**20, bytes_accessed=10 * 2**20, transcendentals=2**20
        ),
        compiler_params=pltpu.CompilerParams(vmem_limit_bytes=BIG),
    )(bank, indices, counts, scalars, powers, early)
    window = jax.ShapeDtypeStruct((2, TPL_DEV, SPAN), jnp.bfloat16)
    own, send = pl.pallas_call(
        filter_kernel,
        out_shape=(window, window),
        in_specs=[SMEM] * 3 + [VMEM] * 4 + [ANY],
        out_specs=(VMEM, VMEM),
        scratch_shapes=[
            pltpu.VMEM((2, DFT_COLS, 256), jnp.float32),
            pltpu.VMEM((2, BATCH * DFT_COLS, 256), jnp.bfloat16),
            pltpu.VMEM((2, BATCH * DFT_COLS, 512), jnp.float32),
            pltpu.VMEM((BATCH, 1024, 256), jnp.bfloat16),
            pltpu.VMEM((4, 2 * COLS * TPL_DEV, 128), jnp.float32),
            pltpu.VMEM((2 * BATCH, 2, DFT_COLS, 256), jnp.bfloat16),
            pltpu.SemaphoreType.DMA((2 * BATCH,)),
        ],
        compiler_params=pltpu.CompilerParams(vmem_limit_bytes=FILTER_VMEM),
    )(indices, counts, half, plane, first_tables, twist, last, waves)
    got = lax.all_gather(send, "det", axis=0)
    out = pl.pallas_call(
        coherent_kernel,
        out_shape=jax.ShapeDtypeStruct((TPL_DEV * SKY, HALF), jnp.float32),
        in_specs=[SMEM] * 4 + [VMEM] * 2,
        out_specs=pl.BlockSpec(memory_space=pl.ANY),
        scratch_shapes=[
            pltpu.VMEM((2 * TPL_DEV * TILES, 128), jnp.float32),
            pltpu.VMEM((2 * TPL_DEV * TILES, 256), jnp.bfloat16),
            pltpu.VMEM((SKY // 2, 256, 256), jnp.bfloat16),
            pltpu.VMEM((TILES, TPL_DEV * SKY, 128), jnp.float32),
            pltpu.SemaphoreType.DMA((TILES,)),
        ],
        compiler_params=pltpu.CompilerParams(vmem_limit_bytes=16 * 1024 * 1024),
    )(half, sky_delay, gain_near, gain_far, own, got)
    return out.reshape(TPL_DEV, SKY, HALF)


def solution(mesh):
    return jax.shard_map(
        on_device,
        mesh=mesh,
        in_specs=(P("det", None, "bank"), P("det", "bank"), P("bank"), P("bank"), P(), P(), P()),
        out_specs=P("bank", None, "det"),
        check_vma=False,
    )
```
